256 devices in a mesh: dp: 32 (over y_lo, z, core), fsdp: 8 (over y_hi, x).
Axes of the slice: x: 4, y: 4 (y_hi: 2, y_lo: 2; y = y_hi * 2 + y_lo), z: 8, core: 2. Of those that a mesh axis runs over, the one named last changes fastest.
Arguments:
- section_input: bfloat16 [32768, 8192], P(('dp', 'fsdp')), may hold values from -24 to 24
- c_weight: bfloat16 [8192, 512], P('fsdp'), may hold values from -0.0625 to 0.0625
- scan_input: bfloat16 [32768, 8192], P(('dp', 'fsdp')), may hold values from -6 to 6
- b_factors: bfloat16 [32768, 512], P(('dp', 'fsdp')), may hold values from -0.5 to 0.5
- step_size: float32 [128, 32768], P(None, ('dp', 'fsdp')), may hold values from 0.5 to 8
- decay_rate: float32 [128], replicated, may hold values from 0.002 to 0.06
- skip_gain: float32 [128], replicated, may hold values from 0.5 to 1.5
- out_grad: bfloat16 [32768, 8192], P(('dp', 'fsdp')), may hold values from -18 to 18
- doc_index: int32 [32768], P(('dp', 'fsdp')), may hold values from 0 to 15, as said below
- kept_rows: int32 [32, 8], P(None, 'fsdp'), may hold values from 16 to 64, as said below
- send_counts: int32 [32, 8, 32], P(None, 'fsdp'), may hold values from 0 to 2, as said below
Outputs:
- input_grad: bfloat16 [32768, 8192], P(('dp', 'fsdp'))
- scan_grad: bfloat16 [32768, 8192], P(('dp', 'fsdp'))
- readout_weight_gradient: float32 [8192, 512], P(('dp', 'fsdp'))
The draws below stay inside these ranges and needn't reach their ends.
Inputs may be any that keep to these rules, and one draw needn't show every extreme that they name: `kept_rows`: rows kept by each device; 64 on every device whose send_counts row is not all zero. send_counts[a, f, b] rows go from dp index a to dp index b in fsdp column f; zero on the diagonal; a device that sends receives nothing; in each column one device sends exactly 2 to every device that receives, and one device receives exactly 32 rows in all, which no device exceeds; kept_rows plus the sends of a device never pass 128. `doc_index`: starts at 0 on each device and never falls within one device's 128 rows; rows of one device with equal numbers form one document.
All inputs are finite; a program needn't handle non-finite values. Where the reference program divides by a largest or mean magnitude, that divisor is 1e-20 or more.
Results may differ from the reference program's by a relative error of at most 0.019.
Values may be sent and summed in bfloat16 or wider, within the bound.
No kernel may reach another device: no remote copies, remote signals or barrier semaphores. Data moves between devices by JAX's collectives and lax.ppermute only.
A program may use at most 128 MiB of HBM per device.

```python
import math
import jax
import jax.numpy as jnp
from jax import lax

D = 8192
HEAD_SUBSET = 128
HDIM = 64
GROUPS = 4
STATE = 128
TOK_DEV = 128
CAP = 2
KEEP = 64
TOKEN_SLOTS = 32768
N_DP = 32
N_FSDP = 8


def route_plan(key):
    heavy_count = N_DP // 2

    def column(column_key):
        order = jax.random.permutation(column_key, N_DP)
        rank = jnp.zeros((N_DP,), jnp.int32).at[order].set(jnp.arange(N_DP, dtype=jnp.int32))
        heavy = rank < heavy_count
        sender_key, keeper_key = jax.random.split(jax.random.fold_in(column_key, 1))
        amounts = CAP - (jax.random.randint(sender_key, (N_DP, N_DP), 0, 4) == 0).astype(jnp.int32)
        pairing = heavy[:, None] & jnp.logical_not(heavy)[None, :]
        full_row = (rank == 0)[:, None]
        full_col = (rank == heavy_count)[None, :]
        amounts = jnp.where(full_row | full_col, CAP, amounts)
        counts = jnp.where(pairing, amounts, 0).astype(jnp.int32)
        light_keep = jax.random.randint(keeper_key, (N_DP,), KEEP // 4, KEEP + 1)
        kept = jnp.where(heavy, KEEP, light_keep).astype(jnp.int32)
        return (kept, counts)
    column_keys = jax.random.split(key, N_FSDP)
    return jax.vmap(column)(column_keys)


def draw_kept_rows(key, part):
    kept, counts = route_plan(key)
    return kept.T


def draw_send_counts(key, part):
    kept, counts = route_plan(key)
    return jnp.transpose(counts, (1, 0, 2))


def draw_doc_index(key, part):
    key = jax.random.fold_in(key, 3)
    block_count = TOKEN_SLOTS // TOK_DEV
    starts = (jax.random.randint(key, (block_count, TOK_DEV), 0, 48) == 0).astype(jnp.int32)
    regular = (jnp.arange(TOK_DEV, dtype=jnp.int32) % 8 == 0).astype(jnp.int32)
    starts = starts.at[0].set(regular)
    starts = starts.at[:, 0].set(0)
    numbers = jnp.cumsum(starts, axis=1)
    numbers = jnp.minimum(numbers, TOK_DEV // 8 - 1)
    return numbers.reshape(TOKEN_SLOTS).astype(jnp.int32)


def draw_step_size(key, part):
    key = jax.random.fold_in(key, 5)
    baseline_key, spike_key = jax.random.split(key)
    baseline_level = jnp.exp(jax.random.uniform(baseline_key, (HEAD_SUBSET, TOKEN_SLOTS), jnp.float32, math.log(0.5), math.log(2.0)))
    spike_level = jax.random.randint(spike_key, (HEAD_SUBSET, TOKEN_SLOTS), 0, 48) == 0
    return jnp.where(spike_level, 4.0 * baseline_level, baseline_level)


def draw_out_grad(key, part):
    key = jax.random.fold_in(key, 7)
    noise_key, scale_key = jax.random.split(key)
    along = jnp.arange(TOKEN_SLOTS, dtype=jnp.float32) / (TOKEN_SLOTS - 1)
    noise = jnp.clip(jax.random.normal(noise_key, (TOKEN_SLOTS, HEAD_SUBSET * HDIM), jnp.float32), -6.0, 6.0)
    rising = jnp.power(3.0, along)
    spread = jnp.exp(jax.random.uniform(scale_key, (TOKEN_SLOTS, 1), jnp.float32, math.log(0.1), 0.0))
    return (noise * (rising[:, None] * spread)).astype(jnp.bfloat16)


def spiked(drawn, stream_key, source, target, blocks, factor):
    def block_of(dim):
        return (jnp.arange(drawn.shape[dim]) // (drawn.shape[dim] // blocks)).reshape((-1,) + (1,) * (drawn.ndim - 1 - dim))

    first = jax.random.permutation(stream_key, blocks)[block_of(target)]
    second = (block_of(target) + blocks // 2) % blocks
    return jnp.where((block_of(source) == first) | (block_of(source) == second), factor * drawn, drawn)


def block_levels(own_key, shape, pieces, least, largest):
    loudness = 1.0
    for dim, shards_of in pieces:
        steps = jax.random.uniform(jax.random.fold_in(jax.random.fold_in(own_key, 6), dim), (shards_of,), jnp.float32, least / len(pieces), largest / len(pieces))
        loudness = loudness * jnp.repeat(jnp.exp(steps), shape[dim] // shards_of).reshape((-1,) + (1,) * (len(shape) - 1 - dim))
    return loudness


def gaussian(own_key, dims, width, limit, shards=(), held_as=jnp.bfloat16):
    result = width * jax.random.normal(own_key, dims, jnp.float32)
    if shards:
        result = result * block_levels(own_key, dims, shards, -0.22, 0.18)
    return jnp.clip(result, -limit, limit).astype(held_as)


def heavy_noise(stream_key, extent, scale, bound, pieces, heavy, kind=jnp.bfloat16):
    entries = scale * jax.random.normal(stream_key, extent, jnp.float32)
    if pieces:
        entries = entries * block_levels(stream_key, extent, pieces, -0.22, 0.18)
    return jnp.clip(spiked(entries, jax.random.fold_in(stream_key, 3), *heavy), -bound, bound).astype(kind)


def setup_inputs(seed: int = 0) -> dict:
    seeds = jax.random.split(jax.random.key(seed), 12)
    section_input = heavy_noise(seeds[0], (TOKEN_SLOTS, D), 1.0, 24.0, ((0, 256),), (0, 1, 256, 6.0))
    c_weight = gaussian(seeds[1], (D, GROUPS * STATE), D ** -0.5, 0.0625, ((0, 8),))
    scan_input = gaussian(seeds[2], (TOKEN_SLOTS, HEAD_SUBSET * HDIM), 1.0, 6.0, ((0, 256),))
    b_factors = gaussian(seeds[3], (TOKEN_SLOTS, GROUPS * STATE), STATE ** -0.5, 0.5, ((0, 256),))
    step_size = draw_step_size(jax.random.fold_in(seeds[11], 71), 0)
    decay_rate = jnp.clip(jnp.exp(jax.random.uniform(seeds[5], (HEAD_SUBSET,), jnp.float32, math.log(0.002), math.log(0.06))), 0.002, 0.06)
    skip_gain = jnp.clip(jax.random.uniform(seeds[6], (HEAD_SUBSET,), jnp.float32, 0.5, 1.5), 0.5, 1.5)
    out_grad = draw_out_grad(jax.random.fold_in(seeds[11], 71), 0)
    doc_index = draw_doc_index(jax.random.fold_in(seeds[11], 71), 0)
    kept_rows = draw_kept_rows(jax.random.fold_in(seeds[11], 71), 0)
    send_counts = draw_send_counts(jax.random.fold_in(seeds[11], 71), 0)
    return dict(section_input=section_input, c_weight=c_weight, scan_input=scan_input, b_factors=b_factors, step_size=step_size, decay_rate=decay_rate, skip_gain=skip_gain, out_grad=out_grad, doc_index=doc_index, kept_rows=kept_rows, send_counts=send_counts)


peak_eps = 1e-6


def scan_block(c_proj, b_factors, scan_input, step_size, decay_rate, skip_gain, out_grad, doc_index, live_len):
    row_count = scan_input.shape[0]
    head_count = step_size.shape[0]
    head_width = scan_input.shape[1] // head_count
    position = jnp.arange(row_count, dtype=jnp.int32)
    live_rows = position < live_len
    grad_live = jnp.where(live_rows[:, None], out_grad, jnp.zeros_like(out_grad))
    same_doc = (doc_index[:, None] == doc_index[None, :]) & (position[None, :] <= position[:, None])
    same_doc = same_doc & live_rows[:, None] & live_rows[None, :]
    totals = jnp.cumsum(step_size * decay_rate[:, None], axis=1)
    gap_sums = totals[:, None, :] - totals[:, :, None]
    decays = jnp.exp(jnp.where(same_doc[None, :, :], gap_sums, jnp.float32(-1e30)))
    grad_heads = grad_live.reshape(row_count, head_count, head_width).astype(jnp.float32)
    x_heads = scan_input.reshape(row_count, head_count, head_width).astype(jnp.float32)
    inner_dots = jnp.einsum("thp,shp->hts", grad_heads, x_heads)
    mixing = (decays * step_size[:, None, :] * inner_dots).reshape(GROUPS, head_count // GROUPS, row_count, row_count)
    mixing = mixing.sum(axis=1).astype(jnp.bfloat16)
    b_groups = b_factors.reshape(row_count, GROUPS, STATE).astype(jnp.float32)
    c_grad = jnp.einsum("gts,sgn->tgn", mixing.astype(jnp.float32), b_groups)
    c_grad = c_grad.reshape(row_count, GROUPS * STATE).astype(jnp.bfloat16)
    c_groups = c_proj.reshape(row_count, GROUPS, STATE).astype(jnp.float32)
    affinity = jnp.einsum("tgn,sgn->gts", c_groups, b_groups)
    kernel = (decays * jnp.repeat(affinity, head_count // GROUPS, axis=0) * step_size[:, None, :]).astype(jnp.bfloat16)
    scan_grad = jnp.einsum("hts,thp->shp", kernel.astype(jnp.float32), grad_heads)
    scan_grad = scan_grad + skip_gain[None, :, None] * grad_heads
    return c_grad, scan_grad.reshape(row_count, head_count * head_width).astype(jnp.bfloat16)


def reference(section_input, c_weight, scan_input, b_factors, step_size, decay_rate, skip_gain, out_grad, doc_index, kept_rows, send_counts):
    block_count = N_DP * N_FSDP
    live_all = (kept_rows + jnp.sum(send_counts, axis=2)).reshape(block_count).astype(jnp.int32)
    input_blocks = section_input.reshape(block_count, TOK_DEV, D)
    scan_blocks = scan_input.reshape(block_count, TOK_DEV, HEAD_SUBSET * HDIM)
    basis_blocks = b_factors.reshape(block_count, TOK_DEV, GROUPS * STATE)
    step_blocks = step_size.reshape(HEAD_SUBSET, block_count, TOK_DEV).transpose(1, 0, 2)
    grad_blocks = out_grad.reshape(block_count, TOK_DEV, HEAD_SUBSET * HDIM)
    doc_blocks = doc_index.reshape(block_count, TOK_DEV)

    def first_pass(item):
        block_in, block_scan, block_basis, block_steps, block_grad, block_docs, block_live = item
        c_proj = jnp.dot(block_in, c_weight, preferred_element_type=jnp.float32).astype(jnp.bfloat16)
        c_grad, scan_grad = scan_block(c_proj, block_basis, block_scan, block_steps, decay_rate, skip_gain, block_grad, block_docs, block_live)
        row_grad = jnp.dot(c_grad, c_weight.T, preferred_element_type=jnp.float32)
        return c_grad, scan_grad, jnp.max(jnp.abs(row_grad))

    readout_gradients, scan_grads, block_tops = lax.map(first_pass, (input_blocks, scan_blocks, basis_blocks, step_blocks, grad_blocks, doc_blocks, live_all))
    row_peak = jnp.max(block_tops)

    def second_pass(block_c):
        row_grad = jnp.dot(block_c, c_weight.T, preferred_element_type=jnp.float32)
        return (row_grad / (row_peak + peak_eps)).astype(jnp.bfloat16)

    input_grad = lax.map(second_pass, readout_gradients).reshape(TOKEN_SLOTS, D)
    flat_c = readout_gradients.reshape(TOKEN_SLOTS, GROUPS * STATE)
    weight_sum = jnp.dot(section_input.T, flat_c, preferred_element_type=jnp.float32)
    readout_weight_gradient = weight_sum / (jnp.max(jnp.abs(weight_sum)) + peak_eps)
    return input_grad, scan_grads.reshape(TOKEN_SLOTS, HEAD_SUBSET * HDIM), readout_weight_gradient
```

```python
import jax
import jax.numpy as jnp
from jax import lax
from jax.experimental import pallas as pl
from jax.experimental.pallas import tpu as pltpu
from jax.sharding import PartitionSpec as P

GROUPS = 4
STATE = 128
HEADS = 128
HDIM = 64
HPG = HEADS // GROUPS
ROWS = 128
LIVE = 96
D = 8192
NARROW = GROUPS * STATE
MEMBERS = 8
CHUNK = D // MEMBERS
LOG2E = 1.4426950408889634
ALL = ("dp", "fsdp")
peak_eps = 1e-06
F32 = jnp.float32
BF16 = jnp.bfloat16


def joint(y_hi, x, y_lo, z, core):
    return (y_lo * 16 + z * 2 + core) * 8 + y_hi * 4 + x


def ring_pairs(dx, flip):
    return [
        (joint(h, x, l, z, c), joint(h ^ flip, (x + dx) % 4, l ^ flip, z, c))
        for h in (0, 1)
        for x in range(4)
        for l in (0, 1)
        for z in range(8)
        for c in (0, 1)
    ]


STEPS = [(0, 0), (1, 0), (3, 0), (2, 0), (0, 1), (1, 1), (3, 1), (2, 1)]
CORE_SWAP = [(i, i ^ 1) for i in range(32)]
SAME_CORE = [[l * 16 + z * 2 + c for l in (0, 1) for z in range(8)] for c in (0, 1)]


def move(value, step):
    return lax.ppermute(value, ALL, ring_pairs(*step))


def pack_kernel(f_ref, s_ref, *out_refs):
    lane = lax.broadcasted_iota(jnp.int32, (LIVE, 128), 1) // 32
    for m, out_ref in enumerate(out_refs):
        f = f_ref[m]
        high, low = f // 4, f % 4

        def tile(o, _):
            acc = None
            for j in range(4):
                start = pl.multiple_of((o * 4 + j) * 256 + high * 128, 128)
                piece = s_ref[:, pl.ds(start, 128)].astype(F32)
                piece = pltpu.roll(piece, (j - low + 4) % 4 * 32, 1)
                acc = piece if acc is None else jnp.where(lane == j, piece, acc)
            out_ref[:, pl.ds(pl.multiple_of(o * 128, 128), 128)] = acc.astype(BF16)
            return 0

        lax.fori_loop(0, CHUNK // 128, tile, 0)


def pack(dests, section_input):
    return pl.pallas_call(
        pack_kernel,
        grid=(1,),
        out_shape=[jax.ShapeDtypeStruct((LIVE, CHUNK), BF16)] * MEMBERS,
        in_specs=[
            pl.BlockSpec(memory_space=pltpu.SMEM),
            pl.BlockSpec((LIVE, D), lambda i: (0, 0)),
        ],
        out_specs=[pl.BlockSpec((LIVE, CHUNK), lambda i: (0, 0))] * MEMBERS,
        compiler_params=pltpu.CompilerParams(vmem_limit_bytes=32 * 2**20),
        cost_estimate=pl.CostEstimate(flops=0, bytes_accessed=4 * LIVE * D, transcendentals=0),
        name="pack",
    )(dests, section_input)


def live_count(me_ref, kept_ref, sends_ref):
    dp = me_ref[0]
    total = kept_ref[dp, 0]
    for b in range(32):
        total = total + sends_ref[dp, b]
    return total


def head_tables(q, rate_ref, step_ref, rate_scr):
    rate_scr[...] = jnp.transpose(jnp.broadcast_to(rate_ref[...], (HEADS, HEADS)))
    steps = step_ref[...]
    totals = steps * rate_scr[pl.ds(pl.multiple_of(q * HPG, HPG), HPG), :]
    lane = lax.broadcasted_iota(jnp.int32, totals.shape, 1)
    reach = 1
    while reach < ROWS:
        totals = totals + jnp.where(lane >= reach, pltpu.roll(totals, reach, 1), 0.0)
        reach *= 2
    totals = totals * LOG2E
    return totals, totals + jnp.log(steps) * LOG2E


def turned(table):
    filler = jnp.zeros((ROWS - HPG, ROWS), F32)
    return jnp.transpose(jnp.concatenate([table, filler], axis=0))


def doc_tables(doc_ref):
    along = jnp.broadcast_to(doc_ref[...].astype(F32), (ROWS, ROWS))
    return along, jnp.transpose(along)


def c_grad_kernel(
    me_ref, kept_ref, sends_ref, rate_ref, doc_ref, step_ref, g_ref, x_ref, b_ref, full_ref, out_ref, rate_scr
):
    q = pl.program_id(0)
    live = live_count(me_ref, kept_ref, sends_ref)
    totals, source = head_tables(q, rate_ref, step_ref, rate_scr)
    totals_col = turned(totals)
    along, down = doc_tables(doc_ref)
    t = lax.broadcasted_iota(jnp.int32, (LIVE, ROWS), 0)
    s = lax.broadcasted_iota(jnp.int32, (LIVE, ROWS), 1)
    keep = (along[:LIVE] == down[:LIVE]) & (s <= t) & (t < live) & (s < live)
    bias = jnp.where(keep, 0.0, -1e30).astype(F32)
    half = lax.broadcasted_iota(jnp.int32, (ROWS, 128), 1) < HDIM
    mixing = jnp.zeros((LIVE, ROWS), F32)
    for p in range(HPG // 2):
        lanes = slice(p * 128, p * 128 + 128)
        x_pair = x_ref[:, lanes]
        zero = jnp.zeros_like(x_pair)
        both = jnp.concatenate([jnp.where(half, x_pair, zero), jnp.where(half, zero, x_pair)], axis=0)
        inner = lax.dot_general(
            g_ref[:, lanes], both, (((1,), (1,)), ((), ())), preferred_element_type=F32
        )
        for k in range(2):
            h = 2 * p + k
            gap = (source[h : h + 1, :] - totals_col[:LIVE, h : h + 1]) + bias
            mixing = mixing + jnp.exp2(gap) * inner[:, k * 128 : k * 128 + 128]
    c_grad = jnp.dot(mixing.astype(BF16), b_ref[...], preferred_element_type=F32).astype(BF16)
    full_ref[:LIVE, :] = c_grad
    full_ref[LIVE:, :] = jnp.zeros((ROWS - LIVE, STATE), BF16)
    out_ref[...] = c_grad


def smem():
    return pl.BlockSpec(memory_space=pltpu.SMEM)


def row_spec():
    return pl.BlockSpec((1, 128), lambda q: (0, 0))


def c_grad_call(me, kept, sends, rate, docs, steps, out_grad, scan_input, b_factors):
    wide = HPG * HDIM
    return pl.pallas_call(
        c_grad_kernel,
        grid=(GROUPS,),
        out_shape=[
            jax.ShapeDtypeStruct((ROWS, NARROW), BF16),
            jax.ShapeDtypeStruct((LIVE, NARROW), BF16),
        ],
        in_specs=[
            smem(),
            smem(),
            smem(),
            row_spec(),
            row_spec(),
            pl.BlockSpec((HPG, ROWS), lambda q: (q, 0)),
            pl.BlockSpec((LIVE, wide), lambda q: (0, q)),
            pl.BlockSpec((ROWS, wide), lambda q: (0, q)),
            pl.BlockSpec((ROWS, STATE), lambda q: (0, q)),
        ],
        out_specs=[
            pl.BlockSpec((ROWS, STATE), lambda q: (0, q)),
            pl.BlockSpec((LIVE, STATE), lambda q: (0, q)),
        ],
        scratch_shapes=[pltpu.VMEM((HEADS, HEADS), F32)],
        compiler_params=pltpu.CompilerParams(vmem_limit_bytes=32 * 2**20),
        cost_estimate=pl.CostEstimate(
            flops=4 * LIVE * ROWS * D, bytes_accessed=4 * ROWS * D, transcendentals=HEADS * LIVE * ROWS
        ),
        name="c_grad",
    )(me, kept, sends, rate, docs, steps, out_grad, scan_input, b_factors)


def scan_grad_kernel(
    me_ref, kept_ref, sends_ref, skip_ref, rate_ref, doc_ref, step_ref, g_ref, c_ref, b_ref, out_ref, rate_scr
):
    q = pl.program_id(0)
    live = live_count(me_ref, kept_ref, sends_ref)
    totals, source = head_tables(q, rate_ref, step_ref, rate_scr)
    source_col = turned(source)
    along, down = doc_tables(doc_ref)
    s = lax.broadcasted_iota(jnp.int32, (LIVE, ROWS), 0)
    t = lax.broadcasted_iota(jnp.int32, (LIVE, ROWS), 1)
    keep = (along[:LIVE] == down[:LIVE]) & (s <= t) & (t < live) & (s < live)
    bias = jnp.where(keep, 0.0, -1e30).astype(F32)
    half = lax.broadcasted_iota(jnp.int32, (ROWS, 128), 1) < HDIM
    affinity = lax.dot_general(
        b_ref[:LIVE, :], c_ref[...], (((1,), (1,)), ((), ())), preferred_element_type=F32
    )
    alive = s < live
    for p in range(HPG // 2):
        lanes = slice(p * 128, p * 128 + 128)
        g_pair = g_ref[:, lanes]
        zero = jnp.zeros_like(g_pair)
        both = jnp.concatenate([jnp.where(half, g_pair, zero), jnp.where(half, zero, g_pair)], axis=0)
        kernels = []
        for k in range(2):
            h = 2 * p + k
            gap = (source_col[:LIVE, h : h + 1] - totals[h : h + 1, :]) + bias
            kernels.append((jnp.exp2(gap) * affinity).astype(BF16))
        grads = jnp.dot(jnp.concatenate(kernels, axis=1), both, preferred_element_type=F32)
        first = q * HPG + 2 * p
        gain = jnp.where(half[:LIVE], skip_ref[first], skip_ref[first + 1])
        grads = grads + jnp.where(alive, gain * g_pair[:LIVE].astype(F32), 0.0)
        out_ref[:LIVE, lanes] = grads.astype(BF16)
    out_ref[LIVE:, :] = jnp.zeros((ROWS - LIVE, HPG * HDIM), BF16)


def scan_grad_call(me, kept, sends, skip, rate, docs, steps, out_grad, c_proj, b_factors):
    wide = HPG * HDIM
    return pl.pallas_call(
        scan_grad_kernel,
        grid=(GROUPS,),
        out_shape=jax.ShapeDtypeStruct((ROWS, D), BF16),
        in_specs=[
            smem(),
            smem(),
            smem(),
            smem(),
            row_spec(),
            row_spec(),
            pl.BlockSpec((HPG, ROWS), lambda q: (q, 0)),
            pl.BlockSpec((ROWS, wide), lambda q: (0, q)),
            pl.BlockSpec((ROWS, STATE), lambda q: (0, q)),
            pl.BlockSpec((ROWS, STATE), lambda q: (0, q)),
        ],
        out_specs=pl.BlockSpec((ROWS, wide), lambda q: (0, q)),
        scratch_shapes=[pltpu.VMEM((HEADS, HEADS), F32)],
        compiler_params=pltpu.CompilerParams(vmem_limit_bytes=32 * 2**20),
        cost_estimate=pl.CostEstimate(
            flops=4 * LIVE * ROWS * D, bytes_accessed=4 * ROWS * D, transcendentals=HEADS * LIVE * ROWS
        ),
        name="scan_grad",
    )(me, kept, sends, skip, rate, docs, steps, out_grad, c_proj, b_factors)


def weight_kernel(me_ref, *refs):
    s_refs, c_refs = refs[:MEMBERS], refs[MEMBERS : 2 * MEMBERS]
    keep_ref, send_ref, s_all, c_all = refs[2 * MEMBERS :]
    for m in range(MEMBERS):
        s_all[m * LIVE : (m + 1) * LIVE, :] = s_refs[m][...]
        c_all[m * LIVE : (m + 1) * LIVE, :] = c_refs[m][...]
    first_core = me_ref[1] == 0
    wide = 256
    for i in range(CHUNK // wide):
        part = lax.dot_general(
            s_all[:, i * wide : (i + 1) * wide],
            c_all[...],
            (((0,), (0,)), ((), ())),
            preferred_element_type=F32,
        )
        for j in range(wide // 64):
            low, high = part[j * 64 : j * 64 + 32], part[j * 64 + 32 : j * 64 + 64]
            keep_ref[i * (wide // 64) + j] = jnp.where(first_core, low, high)
            send_ref[i * (wide // 64) + j] = jnp.where(first_core, high, low).astype(send_ref.dtype)


def weight_call(me, pieces, grads):
    vmem = pl.BlockSpec(memory_space=pltpu.VMEM)
    return pl.pallas_call(
        weight_kernel,
        out_shape=[
            jax.ShapeDtypeStruct((16, 32, NARROW), F32),
            jax.ShapeDtypeStruct((16, 32, NARROW), F32),
        ],
        in_specs=[smem()] + [vmem] * (2 * MEMBERS),
        out_specs=[vmem, vmem],
        scratch_shapes=[
            pltpu.VMEM((MEMBERS * LIVE, CHUNK), BF16),
            pltpu.VMEM((MEMBERS * LIVE, NARROW), BF16),
        ],
        compiler_params=pltpu.CompilerParams(vmem_limit_bytes=32 * 2**20),
        cost_estimate=pl.CostEstimate(
            flops=2 * MEMBERS * LIVE * CHUNK * NARROW, bytes_accessed=7 * 2**20, transcendentals=0
        ),
        name="weight_part",
    )(me, *pieces, *grads)


def shards(
    section_input,
    c_weight,
    scan_input,
    b_factors,
    step_size,
    decay_rate,
    skip_gain,
    out_grad,
    doc_index,
    kept_rows,
    send_counts,
):
    dp_index = lax.axis_index("dp").astype(jnp.int32)
    f_index = lax.axis_index("fsdp").astype(jnp.int32)
    me = jnp.stack([dp_index, dp_index % 2])
    x, y_hi = f_index % 4, f_index // 4
    dests = jnp.stack([(y_hi ^ flip) * 4 + (x + dx) % 4 for dx, flip in STEPS])
    kept = kept_rows.reshape(32, 1)
    sends = send_counts.reshape(32, 32)
    rate, docs = decay_rate.reshape(1, HEADS), doc_index.reshape(1, ROWS)

    weights = lax.all_gather(c_weight, "fsdp", axis=0, tiled=True)

    packed = pack(dests, section_input)
    pieces = [packed[0]] + [move(packed[m], STEPS[m]) for m in range(1, MEMBERS)]

    c_full, c_live = c_grad_call(me, kept, sends, rate, docs, step_size, out_grad, scan_input, b_factors)
    grads = [c_live] + [move(c_live, STEPS[m]) for m in range(1, MEMBERS)]

    mine, theirs = weight_call(me, pieces, grads)
    mine = (mine + lax.ppermute(theirs, "dp", CORE_SWAP)).astype(BF16)
    mine = lax.all_to_all(mine, "dp", 0, 0, axis_index_groups=SAME_CORE)
    weight_sum = jnp.sum(mine.astype(F32), axis=0)

    c_proj = jnp.dot(section_input, weights, preferred_element_type=F32).astype(BF16)
    scan_grad = scan_grad_call(
        me, kept, sends, skip_gain, rate, docs, step_size, out_grad, c_proj, b_factors
    )
    row_grad = lax.dot_general(c_full, weights, (((1,), (1,)), ((), ())), preferred_element_type=F32)

    tops = jnp.where(
        lax.broadcasted_iota(jnp.int32, (256, 1, 128), 2) < 64,
        jnp.max(jnp.abs(row_grad)),
        jnp.max(jnp.abs(weight_sum)),
    )
    tops = jnp.max(lax.all_to_all(tops, ALL, 0, 0), axis=(0, 1))
    input_grad = (row_grad / (tops[0] + peak_eps)).astype(BF16)
    readout_weight_gradient = weight_sum / (tops[64] + peak_eps)
    return (input_grad, scan_grad, readout_weight_gradient)


def solution(mesh):
    rows = P(ALL, None)
    placed = (
        rows,
        P("fsdp", None),
        rows,
        rows,
        P(None, ALL),
        P(),
        P(),
        rows,
        P(ALL),
        P(None, "fsdp"),
        P(None, "fsdp", None),
    )
    return jax.shard_map(
        shards, mesh=mesh, in_specs=placed, out_specs=(rows, rows, rows), check_vma=False
    )
```

```python
import jax
import jax.numpy as jnp
from jax import lax
from jax.experimental import pallas as pl
from jax.experimental.pallas import tpu as pltpu
from jax.sharding import PartitionSpec as P

GROUPS = 4
STATE = 128
HEADS = 128
HDIM = 64
HPG = HEADS // GROUPS
ROWS = 128
LIVE = 96
D = 8192
NARROW = GROUPS * STATE
MEMBERS = 8
CHUNK = D // MEMBERS
BOTH = NARROW + CHUNK
VMEM_LIMIT = 60 * 2**20
LOG2E = 1.4426950408889634
ALL = ("dp", "fsdp")
peak_eps = 1e-06
F32 = jnp.float32
BF16 = jnp.bfloat16


def joint(y_hi, x, y_lo, z, core):
    return (y_lo * 16 + z * 2 + core) * 8 + y_hi * 4 + x


WIDE = [
    [joint(h, x, h ^ s, z, c) for h in (0, 1) for x in range(4)]
    for s in (0, 1)
    for z in range(8)
    for c in (0, 1)
]
def moved(dx, pair):
    return [
        (joint(h, x, l, z, c), joint(h ^ pair, (x + dx) % 4, l ^ pair, z, c))
        for h in (0, 1)
        for x in range(4)
        for l in (0, 1)
        for z in range(8)
        for c in (0, 1)
    ]


X_STEPS = (0, 1, 3, 2)
STEPS = [(dx, pair) for dx in X_STEPS for pair in (0, 1)]
CORE_SWAP = [(i, i ^ 1) for i in range(32)]
SAME_CORE = [[l * 16 + z * 2 + c for l in (0, 1) for z in range(8)] for c in (0, 1)]
HOME = [
    (joint(h, x, l, z, c), joint(z // 4, z % 4, h, 2 * x + l, c))
    for h in (0, 1)
    for x in range(4)
    for l in (0, 1)
    for z in range(8)
    for c in (0, 1)
]


def exchange(value, groups):
    return lax.all_to_all(value, ALL, 0, 0, axis_index_groups=groups)


def along_x(value):
    return [value] + [lax.ppermute(value, ALL, moved(dx, 0)) for dx in X_STEPS[1:]]


def to_pair(value):
    return lax.ppermute(value, ALL, moved(0, 1))


def to_core(value):
    return lax.ppermute(value, "dp", CORE_SWAP)


def coordinates():
    dp, f = lax.axis_index("dp"), lax.axis_index("fsdp")
    return dict(dp=dp, core=dp % 2, y_lo=dp // 16, x=f % 4, y_hi=f // 4)


def rows_at(sign):
    at = coordinates()
    return [(at["y_hi"] + pair) % 2 * 4 + (at["x"] + 4 + sign * dx) % 4 for dx, pair in STEPS]


def sources():
    behind = rows_at(-1)
    return [behind[2 * i : 2 * i + 2] for i in range(4)]


def params():
    return pltpu.CompilerParams(vmem_limit_bytes=VMEM_LIMIT)


def pack_kernel(s_ref, wide_ref):
    wide_ref[0] = s_ref[...]


def pack(section_input):
    return pl.pallas_call(
        pack_kernel,
        grid=(MEMBERS,),
        out_shape=jax.ShapeDtypeStruct((MEMBERS, LIVE, CHUNK), BF16),
        in_specs=[pl.BlockSpec((LIVE, CHUNK), lambda f: (0, f))],
        out_specs=pl.BlockSpec((1, LIVE, CHUNK), lambda f: (f, 0, 0)),
        compiler_params=params(),
        cost_estimate=pl.CostEstimate(flops=0, bytes_accessed=4 * LIVE * D, transcendentals=0),
        name="pack",
    )(section_input)


def live_count(kept_ref, sends_ref):
    own = lax.broadcasted_iota(jnp.int32, (32, 32), 0) == coordinates()["dp"]
    sent = jnp.sum(jnp.where(own, sends_ref[...].astype(F32), 0.0), axis=1, keepdims=True)
    held = jnp.where(own[:, :1], kept_ref[...].astype(F32), 0.0)
    return jnp.sum(sent + held, axis=0, keepdims=True)


def places(shape):
    rows = [lax.broadcasted_iota(jnp.int32, shape, k).astype(F32) for k in range(2)]
    return rows


def head_tables(q, rate_ref, step_ref, rate_scr):
    rate_scr[...] = jnp.transpose(jnp.broadcast_to(rate_ref[...], (HEADS, HEADS)))
    steps = step_ref[...]
    totals = steps * rate_scr[pl.ds(pl.multiple_of(q * HPG, HPG), HPG), :]
    lane = lax.broadcasted_iota(jnp.int32, totals.shape, 1)
    reach = 1
    while reach < ROWS:
        totals = totals + jnp.where(lane >= reach, pltpu.roll(totals, reach, 1), 0.0)
        reach *= 2
    totals = totals * LOG2E
    return totals, totals + jnp.log(steps) * LOG2E


def turned(table):
    filler = jnp.zeros((ROWS - HPG, ROWS), F32)
    return jnp.transpose(jnp.concatenate([table, filler], axis=0))


def doc_tables(doc_ref):
    along = jnp.broadcast_to(doc_ref[...].astype(F32), (ROWS, ROWS))
    return along, jnp.transpose(along)


def c_grad_kernel(
    kept_ref, sends_ref, rate_ref, doc_ref, step_ref, g_ref, x_ref, b_ref, out_ref, rate_scr
):
    q = pl.program_id(0)
    live = live_count(kept_ref, sends_ref)
    totals, source = head_tables(q, rate_ref, step_ref, rate_scr)
    totals_col = turned(totals)
    along, down = doc_tables(doc_ref)
    t, s = places((LIVE, ROWS))
    keep = (along[:LIVE] == down[:LIVE]) & (s <= t) & (t < live) & (s < live)
    bias = jnp.where(keep, 0.0, -1e30).astype(F32)
    half = lax.broadcasted_iota(jnp.int32, (ROWS, 128), 1) < HDIM
    mixing = jnp.zeros((LIVE, ROWS), F32)
    for p in range(HPG // 2):
        lanes = slice(p * 128, p * 128 + 128)
        x_pair = x_ref[:, lanes]
        zero = jnp.zeros_like(x_pair)
        both = jnp.concatenate([jnp.where(half, x_pair, zero), jnp.where(half, zero, x_pair)], axis=0)
        inner = lax.dot_general(
            g_ref[:, lanes], both, (((1,), (1,)), ((), ())), preferred_element_type=F32
        )
        for k in range(2):
            h = 2 * p + k
            gap = (source[h : h + 1, :] - totals_col[:LIVE, h : h + 1]) + bias
            mixing = mixing + jnp.exp2(gap) * inner[:, k * 128 : k * 128 + 128]
    c_grad = jnp.dot(mixing.astype(BF16), b_ref[...], preferred_element_type=F32).astype(BF16)
    out_ref[...] = c_grad


def smem():
    return pl.BlockSpec(memory_space=pltpu.SMEM)


def row_spec():
    return pl.BlockSpec((1, 128), lambda q: (0, 0))


def c_grad_call(kept, sends, rate, docs, steps, out_grad, scan_input, b_factors):
    wide = HPG * HDIM
    return pl.pallas_call(
        c_grad_kernel,
        grid=(GROUPS,),
        out_shape=jax.ShapeDtypeStruct((LIVE, NARROW), BF16),
        in_specs=[
            pl.BlockSpec((32, 1), lambda q: (0, 0)),
            pl.BlockSpec((32, 32), lambda q: (0, 0)),
            row_spec(),
            row_spec(),
            pl.BlockSpec((HPG, ROWS), lambda q: (q, 0)),
            pl.BlockSpec((LIVE, wide), lambda q: (0, q)),
            pl.BlockSpec((ROWS, wide), lambda q: (0, q)),
            pl.BlockSpec((ROWS, STATE), lambda q: (0, q)),
        ],
        out_specs=pl.BlockSpec((LIVE, STATE), lambda q: (0, q)),
        scratch_shapes=[pltpu.VMEM((HEADS, HEADS), F32)],
        compiler_params=params(),
        cost_estimate=pl.CostEstimate(
            flops=4 * LIVE * ROWS * D, bytes_accessed=4 * ROWS * D, transcendentals=HEADS * LIVE * ROWS
        ),
        name="c_grad",
    )(kept, sends, rate, docs, steps, out_grad, scan_input, b_factors)


def scan_grad_kernel(
    kept_ref, sends_ref, skip_ref, rate_ref, doc_ref, step_ref, g_ref, b_ref, *refs
):
    q = pl.program_id(0)
    proj_refs, (out_ref, rate_scr) = refs[:MEMBERS], refs[MEMBERS:]
    live = live_count(kept_ref, sends_ref)
    totals, source = head_tables(q, rate_ref, step_ref, rate_scr)
    source_col = turned(source)
    along, down = doc_tables(doc_ref)
    s, t = places((LIVE, ROWS))
    keep = (along[:LIVE] == down[:LIVE]) & (s <= t) & (t < live) & (s < live)
    bias = jnp.where(keep, 0.0, -1e30).astype(F32)
    half = lax.broadcasted_iota(jnp.int32, (ROWS, 128), 1) < HDIM
    c_proj = proj_refs[0][...].astype(F32)
    for proj_ref in proj_refs[1:]:
        c_proj = c_proj + proj_ref[...].astype(F32)
    c_proj = jnp.concatenate([c_proj.astype(BF16), jnp.zeros((ROWS - LIVE, STATE), BF16)], axis=0)
    affinity = lax.dot_general(
        b_ref[:LIVE, :], c_proj, (((1,), (1,)), ((), ())), preferred_element_type=F32
    )
    alive = s < live
    for p in range(HPG // 2):
        lanes = slice(p * 128, p * 128 + 128)
        g_pair = g_ref[:, lanes]
        zero = jnp.zeros_like(g_pair)
        both = jnp.concatenate([jnp.where(half, g_pair, zero), jnp.where(half, zero, g_pair)], axis=0)
        kernels = []
        for k in range(2):
            h = 2 * p + k
            gap = (source_col[:LIVE, h : h + 1] - totals[h : h + 1, :]) + bias
            kernels.append((jnp.exp2(gap) * affinity).astype(BF16))
        grads = jnp.dot(jnp.concatenate(kernels, axis=1), both, preferred_element_type=F32)
        first = q * HPG + 2 * p
        gain = jnp.where(half[:LIVE], skip_ref[first], skip_ref[first + 1])
        grads = grads + jnp.where(alive, gain * g_pair[:LIVE].astype(F32), 0.0)
        out_ref[:LIVE, lanes] = grads.astype(BF16)
    out_ref[LIVE:, :] = jnp.zeros((ROWS - LIVE, HPG * HDIM), BF16)


def scan_grad_call(kept, sends, skip, rate, docs, steps, out_grad, b_factors, shares):
    wide = HPG * HDIM
    return pl.pallas_call(
        scan_grad_kernel,
        grid=(GROUPS,),
        out_shape=jax.ShapeDtypeStruct((ROWS, D), BF16),
        in_specs=[
            pl.BlockSpec((32, 1), lambda q: (0, 0)),
            pl.BlockSpec((32, 32), lambda q: (0, 0)),
            smem(),
            row_spec(),
            row_spec(),
            pl.BlockSpec((HPG, ROWS), lambda q: (q, 0)),
            pl.BlockSpec((ROWS, wide), lambda q: (0, q)),
            pl.BlockSpec((ROWS, STATE), lambda q: (0, q)),
        ]
        + [pl.BlockSpec((LIVE, STATE), lambda q: (0, q))] * MEMBERS,
        out_specs=pl.BlockSpec((ROWS, wide), lambda q: (0, q)),
        scratch_shapes=[pltpu.VMEM((HEADS, HEADS), F32)],
        compiler_params=params(),
        cost_estimate=pl.CostEstimate(
            flops=4 * LIVE * ROWS * D, bytes_accessed=4 * ROWS * D, transcendentals=HEADS * LIVE * ROWS
        ),
        name="scan_grad",
    )(kept, sends, skip, rate, docs, steps, out_grad, b_factors, *shares)


def gather_grads(c_refs, grads):
    for c_ref, pair in zip(c_refs, sources()):
        for p in range(2):
            grads[pair[p]] = c_ref[p]


def weight_kernel(s_ref, *refs):
    c_refs, (keep_ref, send_ref, grads) = refs[:4], refs[4:]
    gather_grads(c_refs, grads)
    first_core = coordinates()["core"] == 0
    wide = 256
    rows = MEMBERS * LIVE
    for i in range(CHUNK // wide):
        part = lax.dot_general(
            s_ref[:, :, i * wide : (i + 1) * wide].reshape(rows, wide),
            grads[...].reshape(rows, NARROW),
            (((0,), (0,)), ((), ())),
            preferred_element_type=F32,
        ).reshape(8, 32, NARROW)
        place = slice(i // 2 * 8, i // 2 * 8 + 8)

        @pl.when(first_core == (i % 2 == 0))
        def _():
            keep_ref[place] = part

        @pl.when(first_core != (i % 2 == 0))
        def _():
            send_ref[place] = part


def weight_call(pieces, grads):
    vmem = pl.BlockSpec(memory_space=pltpu.VMEM)
    return pl.pallas_call(
        weight_kernel,
        out_shape=[jax.ShapeDtypeStruct((16, 32, NARROW), F32)] * 2,
        in_specs=[vmem] * 5,
        out_specs=[vmem, vmem],
        scratch_shapes=[pltpu.VMEM((MEMBERS, LIVE, NARROW), BF16)],
        compiler_params=params(),
        cost_estimate=pl.CostEstimate(
            flops=2 * MEMBERS * LIVE * CHUNK * NARROW, bytes_accessed=5 * 2**20, transcendentals=0
        ),
        name="weight_part",
    )(pieces, *grads)


def project_kernel(w_ref, s_ref, *refs):
    c_refs, refs = refs[:4], refs[4:]
    out_refs, (top_ref, grads, held) = refs[:MEMBERS], refs[MEMBERS:]
    gather_grads(c_refs, grads)
    rows = MEMBERS * LIVE
    wide = 256
    proj = jnp.dot(s_ref[...].reshape(rows, CHUNK), w_ref[...], preferred_element_type=F32)
    held[:, :, :NARROW] = proj.astype(BF16).reshape(MEMBERS, LIVE, NARROW)
    top = jnp.zeros((8, wide), F32)
    for i in range(CHUNK // wide):
        part = lax.dot_general(
            grads[...].reshape(rows, NARROW),
            w_ref[i * wide : (i + 1) * wide, :],
            (((1,), (1,)), ((), ())),
            preferred_element_type=F32,
        )
        held[:, :, NARROW + i * wide : NARROW + (i + 1) * wide] = part.astype(BF16).reshape(
            MEMBERS, LIVE, wide
        )
        top = jnp.maximum(top, jnp.max(jnp.abs(part).reshape(rows // 8, 8, wide), axis=0))
    for out_ref, f in zip(out_refs, rows_at(1)):
        out_ref[...] = held[f]
    top_ref[...] = jnp.broadcast_to(jnp.max(top), (1, 128))


def project_call(weights, pieces, grads):
    vmem = pl.BlockSpec(memory_space=pltpu.VMEM)
    out = pl.pallas_call(
        project_kernel,
        out_shape=[jax.ShapeDtypeStruct((LIVE, BOTH), BF16)] * MEMBERS
        + [jax.ShapeDtypeStruct((1, 128), F32)],
        in_specs=[vmem] * 6,
        out_specs=[vmem] * 9,
        scratch_shapes=[
            pltpu.VMEM((MEMBERS, LIVE, NARROW), BF16),
            pltpu.VMEM((MEMBERS, LIVE, BOTH), BF16),
        ],
        compiler_params=params(),
        cost_estimate=pl.CostEstimate(
            flops=4 * MEMBERS * LIVE * CHUNK * NARROW, bytes_accessed=6 * 2**20, transcendentals=0
        ),
        name="project",
    )(weights, pieces, *grads)
    return out[:MEMBERS], out[MEMBERS]


def peak_kernel(parts_ref, top_ref, sum_ref, tops_ref):
    total = parts_ref[0].astype(F32)
    for i in range(1, 16):
        total = total + parts_ref[i].astype(F32)
    sum_ref[...] = total
    lane = lax.broadcasted_iota(jnp.int32, (1, 128), 1)
    both = jnp.where(lane < 64, top_ref[...], jnp.max(jnp.abs(total)))
    tops_ref[...] = jnp.broadcast_to(both[None], (256, 1, 128))


def peak_call(parts, top):
    vmem = pl.BlockSpec(memory_space=pltpu.VMEM)
    return pl.pallas_call(
        peak_kernel,
        out_shape=[
            jax.ShapeDtypeStruct((32, NARROW), F32),
            jax.ShapeDtypeStruct((256, 1, 128), F32),
        ],
        in_specs=[vmem, vmem],
        out_specs=[vmem, vmem],
        compiler_params=params(),
        cost_estimate=pl.CostEstimate(flops=16 * 32 * NARROW, bytes_accessed=2**20, transcendentals=0),
        name="peaks",
    )(parts, top)


def finish_kernel(tops_ref, sum_ref, *refs):
    back_refs, (input_ref, weight_ref, held, sems) = refs[:MEMBERS], refs[MEMBERS:]
    tops = jnp.max(tops_ref[...], axis=0)
    scale = 1.0 / (tops[:, :1] + peak_eps)
    copies = []
    for i, (ref, f) in enumerate(zip(back_refs, rows_at(-1))):
        held[i, :LIVE] = (ref[:, NARROW:].astype(F32) * scale).astype(BF16)
        held[i, LIVE:] = jnp.zeros((ROWS - LIVE, CHUNK), BF16)
        columns = pl.ds(pl.multiple_of(f * CHUNK, CHUNK), CHUNK)
        copies.append(pltpu.make_async_copy(held.at[i], input_ref.at[:, columns], sems.at[i]))
        copies[-1].start()
    weight_ref[...] = sum_ref[...] / (tops[:, 64:65] + peak_eps)
    for copy in copies:
        copy.wait()


def finish_call(tops, back, weight_sum):
    vmem = pl.BlockSpec(memory_space=pltpu.VMEM)
    return pl.pallas_call(
        finish_kernel,
        out_shape=[
            jax.ShapeDtypeStruct((ROWS, D), BF16),
            jax.ShapeDtypeStruct((32, NARROW), F32),
        ],
        in_specs=[vmem] * 10,
        out_specs=[pl.BlockSpec(memory_space=pl.ANY), vmem],
        scratch_shapes=[
            pltpu.VMEM((MEMBERS, ROWS, CHUNK), BF16),
            pltpu.SemaphoreType.DMA((MEMBERS,)),
        ],
        compiler_params=params(),
        cost_estimate=pl.CostEstimate(flops=LIVE * D, bytes_accessed=4 * ROWS * D, transcendentals=0),
        name="finish",
    )(tops, weight_sum, *back)


def shards(
    section_input,
    c_weight,
    scan_input,
    b_factors,
    step_size,
    decay_rate,
    skip_gain,
    out_grad,
    doc_index,
    kept_rows,
    send_counts,
):
    kept = kept_rows.reshape(32, 1)
    sends = send_counts.reshape(32, 32)
    rate, docs = decay_rate.reshape(1, HEADS), doc_index.reshape(1, ROWS)

    pieces = exchange(pack(section_input), WIDE)

    c_own = c_grad_call(kept, sends, rate, docs, step_size, out_grad, scan_input, b_factors)
    grads = along_x(jnp.stack([c_own, to_pair(c_own)]))

    keep, send = weight_call(pieces, grads)
    parts = (keep + to_core(send)).astype(BF16)
    parts = lax.all_to_all(parts, "dp", 0, 0, axis_index_groups=SAME_CORE)

    both, top = project_call(c_weight, pieces, grads)
    both = [both[0]] + [lax.ppermute(value, ALL, moved(*step)) for value, step in zip(both[1:], STEPS[1:])]
    weight_sum, tops = peak_call(parts, top)
    tops = exchange(tops, None)
    weight_sum = lax.ppermute(weight_sum, ALL, HOME)
    scan_grad = scan_grad_call(
        kept, sends, skip_gain, rate, docs, step_size, out_grad, b_factors, both
    )
    input_grad, readout_weight_gradient = finish_call(tops, both, weight_sum)
    return (input_grad, scan_grad, readout_weight_gradient)


def solution(mesh):
    rows = P(ALL, None)
    placed = (
        rows,
        P("fsdp", None),
        rows,
        rows,
        P(None, ALL),
        P(),
        P(),
        rows,
        P(ALL),
        P(None, "fsdp"),
        P(None, "fsdp", None),
    )
    return jax.shard_map(
        shards, mesh=mesh, in_specs=placed, out_specs=(rows, rows, rows), check_vma=False
    )
```

```python
import jax
import jax.numpy as jnp
from jax import lax
from jax.experimental import pallas as pl
from jax.experimental.pallas import tpu as pltpu
from jax.sharding import PartitionSpec as P

GROUPS = 4
STATE = 128
HEADS = 128
HDIM = 64
HPG = HEADS // GROUPS
ROWS = 128
LIVE = 96
D = 8192
NARROW = GROUPS * STATE
MEMBERS = 8
CHUNK = D // MEMBERS
BOTH = NARROW + CHUNK
VMEM_LIMIT = 60 * 2**20
LOG2E = 1.4426950408889634
ALL = ("dp", "fsdp")
peak_eps = 1e-06
F32 = jnp.float32
BF16 = jnp.bfloat16


def joint(y_hi, x, y_lo, z, core):
    return (y_lo * 16 + z * 2 + core) * 8 + y_hi * 4 + x


WIDE = [
    [joint(h, x, h ^ s, z, c) for h in (0, 1) for x in range(4)]
    for s in (0, 1)
    for z in range(8)
    for c in (0, 1)
]
def moved(dx, pair):
    return [
        (joint(h, x, l, z, c), joint(h ^ pair, (x + dx) % 4, l ^ pair, z, c))
        for h in (0, 1)
        for x in range(4)
        for l in (0, 1)
        for z in range(8)
        for c in (0, 1)
    ]


X_STEPS = (0, 1, 3, 2)
STEPS = [(dx, pair) for dx in X_STEPS for pair in (0, 1)]
CORE_SWAP = [(i, i ^ 1) for i in range(32)]
SAME_CORE = [[l * 16 + z * 2 + c for l in (0, 1) for z in range(8)] for c in (0, 1)]
HOME = [
    (joint(h, x, l, z, c), joint(z // 4, z % 4, h, 2 * x + l, c))
    for h in (0, 1)
    for x in range(4)
    for l in (0, 1)
    for z in range(8)
    for c in (0, 1)
]


def exchange(value, groups):
    return lax.all_to_all(value, ALL, 0, 0, axis_index_groups=groups)


def along_x(value):
    return [value] + [lax.ppermute(value, ALL, moved(dx, 0)) for dx in X_STEPS[1:]]


def to_pair(value):
    return lax.ppermute(value, ALL, moved(0, 1))


def to_core(value):
    return lax.ppermute(value, "dp", CORE_SWAP)


def coordinates():
    dp, f = lax.axis_index("dp"), lax.axis_index("fsdp")
    return dict(dp=dp, core=dp % 2, y_lo=dp // 16, x=f % 4, y_hi=f // 4)


def rows_at(sign):
    at = coordinates()
    return [(at["y_hi"] + pair) % 2 * 4 + (at["x"] + 4 + sign * dx) % 4 for dx, pair in STEPS]


def sources():
    behind = rows_at(-1)
    return [behind[2 * i : 2 * i + 2] for i in range(4)]


def params(limit=VMEM_LIMIT):
    return pltpu.CompilerParams(vmem_limit_bytes=limit)


def pack_kernel(s_ref, wide_ref, sems):
    copies = [
        pltpu.make_async_copy(
            s_ref.at[pl.ds(0, LIVE), pl.ds(f * CHUNK, CHUNK)], wide_ref.at[f], sems.at[f]
        )
        for f in range(MEMBERS)
    ]
    for copy in copies:
        copy.start()
    for copy in copies:
        copy.wait()


def pack(section_input):
    return pl.pallas_call(
        pack_kernel,
        out_shape=jax.ShapeDtypeStruct((MEMBERS, LIVE, CHUNK), BF16),
        in_specs=[pl.BlockSpec(memory_space=pl.ANY)],
        out_specs=pl.BlockSpec(memory_space=pltpu.VMEM),
        scratch_shapes=[pltpu.SemaphoreType.DMA((MEMBERS,))],
        compiler_params=params(),
        cost_estimate=pl.CostEstimate(flops=0, bytes_accessed=4 * LIVE * D, transcendentals=0),
        name="pack",
    )(section_input)


def live_count(kept_ref, sends_ref):
    dp = coordinates()["dp"]
    row, column = (lax.broadcasted_iota(jnp.int32, (32, 32), k) for k in range(2))
    counts = jnp.where(row == dp, sends_ref[...], 0) + jnp.where(
        (row == 0) & (column == dp), kept_ref[...], 0
    )
    counts = jnp.sum(counts.astype(F32), axis=0, keepdims=True)
    return jnp.sum(counts, axis=1, keepdims=True)


def places(shape):
    rows = [lax.broadcasted_iota(jnp.int32, shape, k).astype(F32) for k in range(2)]
    return rows


def head_tables(rate_ref, step_ref):
    steps = step_ref[...]
    totals = steps * jnp.transpose(jnp.broadcast_to(rate_ref[...], (HEADS, HEADS)))
    lane = lax.broadcasted_iota(jnp.int32, totals.shape, 1)
    reach = 1
    while reach < ROWS:
        totals = totals + jnp.where(lane >= reach, pltpu.roll(totals, reach, 1), 0.0)
        reach *= 2
    totals = totals * LOG2E
    return totals, totals + jnp.log(steps) * LOG2E


def keep_tables(along_ref, down_ref, along, down):
    along_ref[...] = along
    down = jnp.transpose(down)
    for q in range(GROUPS):
        down_ref[q] = pltpu.roll(down, HEADS - q * HPG, 1) if q else down


def row_mask(live, doc_ref, target, source):
    along = jnp.broadcast_to(doc_ref[...].astype(F32), (ROWS, ROWS))
    down = jnp.transpose(along)
    keep = (along[:LIVE] == down[:LIVE]) & (source <= target) & (target < live) & (source < live)
    return jnp.where(keep, 0.0, -1e30).astype(F32)


def group_rows(q):
    return pl.ds(pl.multiple_of(q * HPG, HPG), HPG)


def c_grad_kernel(
    kept_ref, sends_ref, rate_ref, doc_ref, step_ref, g_ref, x_ref, b_ref, out_ref, source_scr, totals_scr, bias_scr
):
    q = pl.program_id(0)

    @pl.when(q == 0)
    def _():
        totals, source = head_tables(rate_ref, step_ref)
        keep_tables(source_scr, totals_scr, source, totals)
        t, s = places((LIVE, ROWS))
        bias_scr[...] = row_mask(live_count(kept_ref, sends_ref), doc_ref, t, s)

    bias = bias_scr[...]
    source = source_scr[group_rows(q), :]
    totals_col = totals_scr[q]
    upper = lax.broadcasted_iota(jnp.int32, (128, ROWS), 0) < HDIM
    mixing = jnp.zeros((LIVE, ROWS), F32)
    for p in range(HPG // 2):
        lanes = slice(p * 128, p * 128 + 128)
        x_pair = x_ref[:, lanes]
        zero = jnp.zeros_like(x_pair)
        x_turned = jnp.transpose(x_pair)
        both = jnp.concatenate([jnp.where(upper, x_turned, zero), jnp.where(upper, zero, x_turned)], axis=1)
        inner = jnp.dot(g_ref[:, lanes], both, preferred_element_type=F32)
        for k in range(2):
            h = 2 * p + k
            gap = (source[h : h + 1, :] - totals_col[:LIVE, h : h + 1]) + bias
            mixing = mixing + jnp.exp2(gap) * inner[:, k * 128 : k * 128 + 128]
    c_grad = jnp.dot(mixing.astype(BF16), b_ref[...], preferred_element_type=F32).astype(BF16)
    out_ref[...] = c_grad


def smem():
    return pl.BlockSpec(memory_space=pltpu.SMEM)


def row_spec():
    return pl.BlockSpec((1, 128), lambda q: (0, 0))


def c_grad_call(kept, sends, rate, docs, steps, out_grad, scan_input, b_factors):
    wide = HPG * HDIM
    return pl.pallas_call(
        c_grad_kernel,
        grid=(GROUPS,),
        out_shape=jax.ShapeDtypeStruct((LIVE, NARROW), BF16),
        in_specs=[
            pl.BlockSpec((1, 32), lambda q: (0, 0)),
            pl.BlockSpec((32, 32), lambda q: (0, 0)),
            row_spec(),
            row_spec(),
            pl.BlockSpec((HEADS, ROWS), lambda q: (0, 0)),
            pl.BlockSpec((LIVE, wide), lambda q: (0, q)),
            pl.BlockSpec((ROWS, wide), lambda q: (0, q)),
            pl.BlockSpec((ROWS, STATE), lambda q: (0, q)),
        ],
        out_specs=pl.BlockSpec((LIVE, STATE), lambda q: (0, q)),
        scratch_shapes=[
            pltpu.VMEM((HEADS, ROWS), F32),
            pltpu.VMEM((GROUPS, ROWS, HEADS), F32),
            pltpu.VMEM((LIVE, ROWS), F32),
        ],
        compiler_params=params(),
        cost_estimate=pl.CostEstimate(
            flops=4 * LIVE * ROWS * D, bytes_accessed=4 * ROWS * D, transcendentals=HEADS * LIVE * ROWS
        ),
        name="c_grad",
    )(kept, sends, rate, docs, steps, out_grad, scan_input, b_factors)


def scan_grad_kernel(
    kept_ref, sends_ref, skip_ref, rate_ref, doc_ref, step_ref, g_ref, b_ref, *refs
):
    q = pl.program_id(0)
    proj_refs, both_refs, refs = refs[:MEMBERS], refs[MEMBERS : 2 * MEMBERS], refs[2 * MEMBERS :]
    out_ref, back_ref, totals_scr, source_scr, bias_scr, live_scr, sems = refs
    copies = [
        pltpu.make_async_copy(ref.at[:, pl.ds(NARROW, CHUNK)], back_ref.at[f], sems.at[i])
        for i, (ref, f) in enumerate(zip(both_refs, rows_at(-1)))
    ]

    @pl.when(q == 0)
    def _():
        for copy in copies:
            copy.start()
        totals, source = head_tables(rate_ref, step_ref)
        keep_tables(totals_scr, source_scr, totals, source)
        s, t = places((LIVE, ROWS))
        live = live_count(kept_ref, sends_ref)
        bias_scr[...] = row_mask(live, doc_ref, t, s)
        live_scr[...] = jnp.where(s < live, 1.0, 0.0)

    bias = bias_scr[...]
    totals = totals_scr[group_rows(q), :]
    source_col = source_scr[q]
    half = lax.broadcasted_iota(jnp.int32, (ROWS, 128), 1) < HDIM
    c_proj = proj_refs[0][...].astype(F32)
    for proj_ref in proj_refs[1:]:
        c_proj = c_proj + proj_ref[...].astype(F32)
    c_proj = jnp.concatenate([c_proj.astype(BF16), jnp.zeros((ROWS - LIVE, STATE), BF16)], axis=0)
    affinity = lax.dot_general(
        b_ref[:LIVE, :], c_proj, (((1,), (1,)), ((), ())), preferred_element_type=F32
    )
    alive = live_scr[...]
    for p in range(HPG // 2):
        lanes = slice(p * 128, p * 128 + 128)
        g_pair = g_ref[:, lanes]
        zero = jnp.zeros_like(g_pair)
        both = jnp.concatenate([jnp.where(half, g_pair, zero), jnp.where(half, zero, g_pair)], axis=0)
        kernels = []
        for k in range(2):
            h = 2 * p + k
            gap = (source_col[:LIVE, h : h + 1] - totals[h : h + 1, :]) + bias
            kernels.append((jnp.exp2(gap) * affinity).astype(BF16))
        grads = jnp.dot(jnp.concatenate(kernels, axis=1), both, preferred_element_type=F32)
        first = q * HPG + 2 * p
        gain = jnp.where(half[:LIVE], skip_ref[first], skip_ref[first + 1]) * alive
        grads = grads + gain * g_pair[:LIVE].astype(F32)
        out_ref[:LIVE, lanes] = grads.astype(BF16)
    out_ref[LIVE:, :] = jnp.zeros((ROWS - LIVE, HPG * HDIM), BF16)

    @pl.when(q == GROUPS - 1)
    def _():
        for copy in copies:
            copy.wait()


def scan_grad_call(kept, sends, skip, rate, docs, steps, out_grad, b_factors, shares):
    wide = HPG * HDIM
    return pl.pallas_call(
        scan_grad_kernel,
        grid=(GROUPS,),
        out_shape=[
            jax.ShapeDtypeStruct((ROWS, D), BF16),
            jax.ShapeDtypeStruct((MEMBERS, LIVE, CHUNK), BF16),
        ],
        in_specs=[
            pl.BlockSpec((1, 32), lambda q: (0, 0)),
            pl.BlockSpec((32, 32), lambda q: (0, 0)),
            smem(),
            row_spec(),
            row_spec(),
            pl.BlockSpec((HEADS, ROWS), lambda q: (0, 0)),
            pl.BlockSpec((ROWS, wide), lambda q: (0, q)),
            pl.BlockSpec((ROWS, STATE), lambda q: (0, q)),
        ]
        + [pl.BlockSpec((LIVE, STATE), lambda q: (0, q))] * MEMBERS
        + [pl.BlockSpec(memory_space=pl.ANY)] * MEMBERS,
        out_specs=[
            pl.BlockSpec((ROWS, wide), lambda q: (0, q)),
            pl.BlockSpec((MEMBERS, LIVE, CHUNK), lambda q: (0, 0, 0)),
        ],
        scratch_shapes=[
            pltpu.VMEM((HEADS, ROWS), F32),
            pltpu.VMEM((GROUPS, ROWS, HEADS), F32),
            pltpu.VMEM((LIVE, ROWS), F32),
            pltpu.VMEM((LIVE, ROWS), F32),
            pltpu.SemaphoreType.DMA((MEMBERS,)),
        ],
        compiler_params=params(),
        cost_estimate=pl.CostEstimate(
            flops=4 * LIVE * ROWS * D, bytes_accessed=4 * ROWS * D, transcendentals=HEADS * LIVE * ROWS
        ),
        name="scan_grad",
    )(kept, sends, skip, rate, docs, steps, out_grad, b_factors, *shares, *shares)


def weight_kernel(s_ref, *refs):
    c_refs, (keep_ref, send_ref, grads) = refs[:MEMBERS], refs[MEMBERS:]
    for c_ref, f in zip(c_refs, rows_at(-1)):
        grads[f] = c_ref[...]
    first_core = coordinates()["core"] == 0
    wide = 256
    rows = MEMBERS * LIVE
    for i in range(CHUNK // wide):
        part = lax.dot_general(
            s_ref[:, :, i * wide : (i + 1) * wide].reshape(rows, wide),
            grads[...].reshape(rows, NARROW),
            (((0,), (0,)), ((), ())),
            preferred_element_type=F32,
        ).reshape(8, 32, NARROW)
        place = slice(i // 2 * 8, i // 2 * 8 + 8)

        @pl.when(first_core == (i % 2 == 0))
        def _():
            keep_ref[place] = part

        @pl.when(first_core != (i % 2 == 0))
        def _():
            send_ref[place] = part.astype(BF16)


def weight_call(pieces, grads):
    vmem = pl.BlockSpec(memory_space=pltpu.VMEM)
    return pl.pallas_call(
        weight_kernel,
        out_shape=[jax.ShapeDtypeStruct((16, 32, NARROW), kind) for kind in (F32, BF16)]
        + [jax.ShapeDtypeStruct((MEMBERS, LIVE, NARROW), BF16)],
        in_specs=[vmem] * 9,
        out_specs=[vmem] * 3,
        compiler_params=params(24 * 2**20),
        cost_estimate=pl.CostEstimate(
            flops=2 * MEMBERS * LIVE * CHUNK * NARROW, bytes_accessed=5 * 2**20, transcendentals=0
        ),
        name="weight_part",
    )(pieces, *grads)


def project_kernel(w_ref, s_ref, grads, *refs):
    out_refs, (top_ref, held) = refs[:MEMBERS], refs[MEMBERS:]
    rows = MEMBERS * LIVE
    wide = 256
    proj = jnp.dot(s_ref[...].reshape(rows, CHUNK), w_ref[...], preferred_element_type=F32)
    held[:, :, :NARROW] = proj.astype(BF16).reshape(MEMBERS, LIVE, NARROW)
    top = jnp.zeros((8, wide), F32)
    for i in range(CHUNK // wide):
        part = lax.dot_general(
            grads[...].reshape(rows, NARROW),
            w_ref[i * wide : (i + 1) * wide, :],
            (((1,), (1,)), ((), ())),
            preferred_element_type=F32,
        )
        held[:, :, NARROW + i * wide : NARROW + (i + 1) * wide] = part.astype(BF16).reshape(
            MEMBERS, LIVE, wide
        )
        top = jnp.maximum(top, jnp.max(jnp.abs(part).reshape(rows // 8, 8, wide), axis=0))
    for out_ref, f in zip(out_refs, rows_at(1)):
        out_ref[...] = held[f]
    top_ref[...] = jnp.broadcast_to(jnp.max(top), (1, 128))


def project_call(weights, pieces, grads):
    vmem = pl.BlockSpec(memory_space=pltpu.VMEM)
    out = pl.pallas_call(
        project_kernel,
        out_shape=[jax.ShapeDtypeStruct((LIVE, BOTH), BF16)] * MEMBERS
        + [jax.ShapeDtypeStruct((1, 128), F32)],
        in_specs=[vmem] * 3,
        out_specs=[vmem] * 9,
        scratch_shapes=[
            pltpu.VMEM((MEMBERS, LIVE, BOTH), BF16),
        ],
        compiler_params=params(24 * 2**20),
        cost_estimate=pl.CostEstimate(
            flops=4 * MEMBERS * LIVE * CHUNK * NARROW, bytes_accessed=6 * 2**20, transcendentals=0
        ),
        name="project",
    )(weights, pieces, grads)
    return out[:MEMBERS], out[MEMBERS]


def peak_kernel(parts_ref, top_ref, sum_ref, tops_ref):
    total = parts_ref[0].astype(F32)
    for i in range(1, 16):
        total = total + parts_ref[i].astype(F32)
    sum_ref[...] = total
    lane = lax.broadcasted_iota(jnp.int32, (1, 128), 1)
    both = jnp.where(lane < 64, top_ref[...], jnp.max(jnp.abs(total)))
    tops_ref[...] = jnp.broadcast_to(both[None], (256, 1, 128))


def peak_call(parts, top):
    vmem = pl.BlockSpec(memory_space=pltpu.VMEM)
    return pl.pallas_call(
        peak_kernel,
        out_shape=[
            jax.ShapeDtypeStruct((32, NARROW), F32),
            jax.ShapeDtypeStruct((256, 1, 128), F32),
        ],
        in_specs=[vmem, vmem],
        out_specs=[vmem, vmem],
        compiler_params=params(16 * 2**20),
        cost_estimate=pl.CostEstimate(flops=16 * 32 * NARROW, bytes_accessed=2**20, transcendentals=0),
        name="peaks",
    )(parts, top)


def finish_kernel(tops_ref, sum_ref, back_ref, input_ref, weight_ref, held, sems):
    tops = jnp.max(tops_ref[...], axis=0)
    scale = 1.0 / (tops[:, :1] + peak_eps)
    held[:, LIVE:, :] = jnp.zeros((MEMBERS, ROWS - LIVE, CHUNK), BF16)
    copies = []
    for f in range(MEMBERS):
        held[f, :LIVE] = (back_ref[f].astype(F32) * scale).astype(BF16)
        columns = pl.ds(f * CHUNK, CHUNK)
        copies.append(pltpu.make_async_copy(held.at[f], input_ref.at[:, columns], sems.at[f]))
        copies[-1].start()
    weight_ref[...] = sum_ref[...] / (tops[:, 64:65] + peak_eps)
    for copy in copies:
        copy.wait()


def finish_call(tops, back, weight_sum):
    vmem = pl.BlockSpec(memory_space=pltpu.VMEM)
    return pl.pallas_call(
        finish_kernel,
        out_shape=[
            jax.ShapeDtypeStruct((ROWS, D), BF16),
            jax.ShapeDtypeStruct((32, NARROW), F32),
        ],
        in_specs=[vmem] * 3,
        out_specs=[pl.BlockSpec(memory_space=pl.ANY), vmem],
        scratch_shapes=[
            pltpu.VMEM((MEMBERS, ROWS, CHUNK), BF16),
            pltpu.SemaphoreType.DMA((MEMBERS,)),
        ],
        compiler_params=params(16 * 2**20),
        cost_estimate=pl.CostEstimate(flops=LIVE * D, bytes_accessed=4 * ROWS * D, transcendentals=0),
        name="finish",
    )(tops, weight_sum, back)


def shards(
    section_input,
    c_weight,
    scan_input,
    b_factors,
    step_size,
    decay_rate,
    skip_gain,
    out_grad,
    doc_index,
    kept_rows,
    send_counts,
):
    kept = kept_rows.reshape(1, 32)
    sends = send_counts.reshape(32, 32)
    rate, docs = decay_rate.reshape(1, HEADS), doc_index.reshape(1, ROWS)

    pieces = exchange(pack(section_input), WIDE)

    c_own = c_grad_call(kept, sends, rate, docs, step_size, out_grad, scan_input, b_factors)
    grads = [c_own] + [lax.ppermute(c_own, ALL, moved(*step)) for step in STEPS[1:]]

    keep, send, grads = weight_call(pieces, grads)
    parts = (keep + to_core(send).astype(F32)).astype(BF16)
    parts = lax.all_to_all(parts, "dp", 0, 0, axis_index_groups=SAME_CORE)

    both, top = project_call(c_weight, pieces, grads)
    both = [both[0]] + [lax.ppermute(value, ALL, moved(*step)) for value, step in zip(both[1:], STEPS[1:])]
    weight_sum, tops = peak_call(parts, top)
    tops = exchange(tops, None)
    weight_sum = lax.ppermute(weight_sum, ALL, HOME)
    scan_grad, back = scan_grad_call(
        kept, sends, skip_gain, rate, docs, step_size, out_grad, b_factors, both
    )
    input_grad, readout_weight_gradient = finish_call(tops, back, weight_sum)
    return (input_grad, scan_grad, readout_weight_gradient)


def solution(mesh):
    rows = P(ALL, None)
    placed = (
        rows,
        P("fsdp", None),
        rows,
        rows,
        P(None, ALL),
        P(),
        P(),
        rows,
        P(ALL),
        P(None, "fsdp"),
        P(None, "fsdp", None),
    )
    return jax.shard_map(
        shards, mesh=mesh, in_specs=placed, out_specs=(rows, rows, rows), check_vma=False
    )
```

```python
import jax
import jax.numpy as jnp
from jax import lax
from jax.experimental import pallas as pl
from jax.experimental.pallas import tpu as pltpu
from jax.sharding import PartitionSpec as P

GROUPS = 4
STATE = 128
HEADS = 128
HDIM = 64
HPG = HEADS // GROUPS
ROWS = 128
LIVE = 96
D = 8192
NARROW = GROUPS * STATE
MEMBERS = 8
CHUNK = D // MEMBERS
BOTH = NARROW + CHUNK
VMEM_LIMIT = 60 * 2**20
LOG2E = 1.4426950408889634
ALL = ("dp", "fsdp")
peak_eps = 1e-06
F32 = jnp.float32
BF16 = jnp.bfloat16


def joint(y_hi, x, y_lo, z, core):
    return (y_lo * 16 + z * 2 + core) * 8 + y_hi * 4 + x


WIDE = [
    [joint(h, x, h ^ s, z, c) for h in (0, 1) for x in range(4)]
    for s in (0, 1)
    for z in range(8)
    for c in (0, 1)
]
def moved(dx, pair):
    return [
        (joint(h, x, l, z, c), joint(h ^ pair, (x + dx) % 4, l ^ pair, z, c))
        for h in (0, 1)
        for x in range(4)
        for l in (0, 1)
        for z in range(8)
        for c in (0, 1)
    ]


STEPS = [(0, 0), (2, 1), (2, 0), (1, 1), (3, 1), (0, 1), (1, 0), (3, 0)]
CORE_SWAP = [(i, i ^ 1) for i in range(32)]
SAME_CORE = [[l * 16 + z * 2 + c for l in (0, 1) for z in range(8)] for c in (0, 1)]
AWAY = (3, 2, 0, 1)


def summed_at(x, b, x_home):
    away = AWAY[(x_home - x) % 4]
    return (2 * x + 1 + away) % 8 if b else (2 * x - away) % 8


HOME = [
    (joint(h, x, k, summed_at(x, b, i), c), joint(k, i, h, 2 * x + b, c))
    for h in (0, 1)
    for x in range(4)
    for k in (0, 1)
    for i in range(4)
    for b in (0, 1)
    for c in (0, 1)
]


def exchange(value, groups):
    return lax.all_to_all(value, ALL, 0, 0, axis_index_groups=groups)


def to_core(value):
    return lax.ppermute(value, "dp", CORE_SWAP)


def coordinates():
    dp, f = lax.axis_index("dp"), lax.axis_index("fsdp")
    return dict(dp=dp, core=dp % 2, y_lo=dp // 16, x=f % 4, y_hi=f // 4)


def rows_at(sign):
    at = coordinates()
    return [(at["y_hi"] + pair) % 2 * 4 + (at["x"] + 4 + sign * dx) % 4 for dx, pair in STEPS]


def params(limit=VMEM_LIMIT):
    return pltpu.CompilerParams(vmem_limit_bytes=limit)


def pack_kernel(s_ref, wide_ref, sems):
    copies = [
        pltpu.make_async_copy(
            s_ref.at[pl.ds(0, LIVE), pl.ds(f * CHUNK, CHUNK)], wide_ref.at[f], sems.at[f]
        )
        for f in range(MEMBERS)
    ]
    for copy in copies:
        copy.start()
    for copy in copies:
        copy.wait()


def pack(section_input):
    return pl.pallas_call(
        pack_kernel,
        out_shape=jax.ShapeDtypeStruct((MEMBERS, LIVE, CHUNK), BF16),
        in_specs=[pl.BlockSpec(memory_space=pl.ANY)],
        out_specs=pl.BlockSpec(memory_space=pltpu.VMEM),
        scratch_shapes=[pltpu.SemaphoreType.DMA((MEMBERS,))],
        compiler_params=params(),
        cost_estimate=pl.CostEstimate(flops=0, bytes_accessed=4 * LIVE * D, transcendentals=0),
        name="pack",
    )(section_input)


def live_count(kept_ref, sends_ref):
    dp = coordinates()["dp"]
    row, column = (lax.broadcasted_iota(jnp.int32, (32, 32), k) for k in range(2))
    counts = jnp.where(row == dp, sends_ref[...], 0) + jnp.where(
        (row == 0) & (column == dp), kept_ref[...], 0
    )
    counts = jnp.sum(counts.astype(F32), axis=0, keepdims=True)
    return jnp.sum(counts, axis=1, keepdims=True)


def places(shape):
    rows = [lax.broadcasted_iota(jnp.int32, shape, k).astype(F32) for k in range(2)]
    return rows


def head_tables(rate_ref, step_ref):
    steps = step_ref[...]
    totals = steps * jnp.transpose(jnp.broadcast_to(rate_ref[...], (HEADS, HEADS)))
    lane = lax.broadcasted_iota(jnp.int32, totals.shape, 1)
    reach = 1
    while reach < ROWS:
        totals = totals + jnp.where(lane >= reach, pltpu.roll(totals, reach, 1), 0.0)
        reach *= 2
    totals = totals * LOG2E
    return totals, totals + jnp.log(steps) * LOG2E


def keep_tables(along_ref, down_ref, along, down):
    along_ref[...] = along
    down = jnp.transpose(down)
    for q in range(GROUPS):
        down_ref[q] = pltpu.roll(down, HEADS - q * HPG, 1) if q else down


def row_mask(live, doc_ref, target, source):
    along = jnp.broadcast_to(doc_ref[...].astype(F32), (ROWS, ROWS))
    down = jnp.transpose(along)
    keep = (along[:LIVE] == down[:LIVE]) & (source <= target) & (target < live) & (source < live)
    return jnp.where(keep, 0.0, -1e30).astype(F32)


def group_rows(q):
    return pl.ds(pl.multiple_of(q * HPG, HPG), HPG)


def c_grad_kernel(
    kept_ref, sends_ref, rate_ref, doc_ref, step_ref, g_ref, x_ref, b_ref, out_ref, source_scr, totals_scr, bias_scr
):
    q = pl.program_id(0)

    @pl.when(q == 0)
    def _():
        totals, source = head_tables(rate_ref, step_ref)
        keep_tables(source_scr, totals_scr, source, totals)
        t, s = places((LIVE, ROWS))
        bias_scr[...] = row_mask(live_count(kept_ref, sends_ref), doc_ref, t, s)

    bias = bias_scr[...]
    source = source_scr[group_rows(q), :]
    totals_col = totals_scr[q]
    upper = lax.broadcasted_iota(jnp.int32, (128, ROWS), 0) < HDIM
    mixing = jnp.zeros((LIVE, ROWS), F32)
    for p in range(HPG // 2):
        lanes = slice(p * 128, p * 128 + 128)
        x_pair = x_ref[:, lanes]
        zero = jnp.zeros_like(x_pair)
        x_turned = jnp.transpose(x_pair)
        both = jnp.concatenate([jnp.where(upper, x_turned, zero), jnp.where(upper, zero, x_turned)], axis=1)
        inner = jnp.dot(g_ref[:, lanes], both, preferred_element_type=F32)
        for k in range(2):
            h = 2 * p + k
            gap = (source[h : h + 1, :] - totals_col[:LIVE, h : h + 1]) + bias
            mixing = mixing + jnp.exp2(gap) * inner[:, k * 128 : k * 128 + 128]
    c_grad = jnp.dot(mixing.astype(BF16), b_ref[...], preferred_element_type=F32).astype(BF16)
    out_ref[...] = c_grad


def smem():
    return pl.BlockSpec(memory_space=pltpu.SMEM)


def row_spec():
    return pl.BlockSpec((1, 128), lambda q: (0, 0))


def c_grad_call(kept, sends, rate, docs, steps, out_grad, scan_input, b_factors):
    wide = HPG * HDIM
    return pl.pallas_call(
        c_grad_kernel,
        grid=(GROUPS,),
        out_shape=pltpu.VMEM((LIVE, NARROW), BF16),
        in_specs=[
            pl.BlockSpec((1, 32), lambda q: (0, 0)),
            pl.BlockSpec((32, 32), lambda q: (0, 0)),
            row_spec(),
            row_spec(),
            pl.BlockSpec((HEADS, ROWS), lambda q: (0, 0)),
            pl.BlockSpec((LIVE, wide), lambda q: (0, q)),
            pl.BlockSpec((ROWS, wide), lambda q: (0, q)),
            pl.BlockSpec((ROWS, STATE), lambda q: (0, q)),
        ],
        out_specs=pl.BlockSpec((LIVE, STATE), lambda q: (0, q)),
        scratch_shapes=[
            pltpu.VMEM((HEADS, ROWS), F32),
            pltpu.VMEM((GROUPS, ROWS, HEADS), F32),
            pltpu.VMEM((LIVE, ROWS), F32),
        ],
        compiler_params=params(),
        cost_estimate=pl.CostEstimate(
            flops=4 * LIVE * ROWS * D, bytes_accessed=4 * ROWS * D, transcendentals=HEADS * LIVE * ROWS
        ),
        name="c_grad",
    )(kept, sends, rate, docs, steps, out_grad, scan_input, b_factors)


def scan_grad_kernel(
    kept_ref, sends_ref, skip_ref, rate_ref, doc_ref, step_ref, g_ref, b_ref, *refs
):
    q = pl.program_id(0)
    proj_refs, (out_ref, totals_scr, source_scr, bias_scr, live_scr) = refs[:MEMBERS], refs[MEMBERS:]

    @pl.when(q == 0)
    def _():
        totals, source = head_tables(rate_ref, step_ref)
        keep_tables(totals_scr, source_scr, totals, source)
        s, t = places((LIVE, ROWS))
        live = live_count(kept_ref, sends_ref)
        bias_scr[...] = row_mask(live, doc_ref, t, s)
        live_scr[...] = jnp.where(s < live, 1.0, 0.0)

    bias = bias_scr[...]
    totals = totals_scr[group_rows(q), :]
    source_col = source_scr[q]
    half = lax.broadcasted_iota(jnp.int32, (ROWS, 128), 1) < HDIM
    c_proj = proj_refs[0][...].astype(F32)
    for proj_ref in proj_refs[1:]:
        c_proj = c_proj + proj_ref[...].astype(F32)
    c_proj = jnp.concatenate([c_proj.astype(BF16), jnp.zeros((ROWS - LIVE, STATE), BF16)], axis=0)
    affinity = lax.dot_general(
        b_ref[:LIVE, :], c_proj, (((1,), (1,)), ((), ())), preferred_element_type=F32
    )
    alive = live_scr[...]
    for p in range(HPG // 2):
        lanes = slice(p * 128, p * 128 + 128)
        g_pair = g_ref[:, lanes]
        zero = jnp.zeros_like(g_pair)
        both = jnp.concatenate([jnp.where(half, g_pair, zero), jnp.where(half, zero, g_pair)], axis=0)
        kernels = []
        for k in range(2):
            h = 2 * p + k
            gap = (source_col[:LIVE, h : h + 1] - totals[h : h + 1, :]) + bias
            kernels.append((jnp.exp2(gap) * affinity).astype(BF16))
        grads = jnp.dot(jnp.concatenate(kernels, axis=1), both, preferred_element_type=F32)
        first = q * HPG + 2 * p
        gain = jnp.where(half[:LIVE], skip_ref[first], skip_ref[first + 1]) * alive
        grads = grads + gain * g_pair[:LIVE].astype(F32)
        out_ref[:LIVE, lanes] = grads.astype(BF16)
    out_ref[LIVE:, :] = jnp.zeros((ROWS - LIVE, HPG * HDIM), BF16)


def scan_grad_call(kept, sends, skip, rate, docs, steps, out_grad, b_factors, shares):
    wide = HPG * HDIM
    return pl.pallas_call(
        scan_grad_kernel,
        grid=(GROUPS,),
        out_shape=jax.ShapeDtypeStruct((ROWS, D), BF16),
        in_specs=[
            pl.BlockSpec((1, 32), lambda q: (0, 0)),
            pl.BlockSpec((32, 32), lambda q: (0, 0)),
            smem(),
            row_spec(),
            row_spec(),
            pl.BlockSpec((HEADS, ROWS), lambda q: (0, 0)),
            pl.BlockSpec((ROWS, wide), lambda q: (0, q)),
            pl.BlockSpec((ROWS, STATE), lambda q: (0, q)),
        ]
        + [pl.BlockSpec((LIVE, STATE), lambda q: (0, q))] * MEMBERS,
        out_specs=pl.BlockSpec((ROWS, wide), lambda q: (0, q)),
        scratch_shapes=[
            pltpu.VMEM((HEADS, ROWS), F32),
            pltpu.VMEM((GROUPS, ROWS, HEADS), F32),
            pltpu.VMEM((LIVE, ROWS), F32),
            pltpu.VMEM((LIVE, ROWS), F32),
        ],
        compiler_params=params(),
        cost_estimate=pl.CostEstimate(
            flops=4 * LIVE * ROWS * D, bytes_accessed=4 * ROWS * D, transcendentals=HEADS * LIVE * ROWS
        ),
        name="scan_grad",
    )(kept, sends, skip, rate, docs, steps, out_grad, b_factors, *shares)


def weight_kernel(s_ref, *refs):
    c_refs, (keep_ref, send_ref, grads) = refs[:MEMBERS], refs[MEMBERS:]
    for c_ref, f in zip(c_refs, rows_at(-1)):
        grads[f] = c_ref[...]
    at = coordinates()
    first_core = at["core"] == 0

    def place(b, j):
        step = (j % 4 + 4 - at["x"]) % 4
        away = jnp.where(step == 0, AWAY[0], jnp.where(step == 1, AWAY[1], jnp.where(step == 2, AWAY[2], AWAY[3])))
        z = 2 * at["x"] + 1 + away if b else 2 * at["x"] + 8 - away
        return j // 4 * 8 + z % 8

    wide = 256
    rows = MEMBERS * LIVE
    for i in range(CHUNK // wide):
        part = lax.dot_general(
            s_ref[:, :, i * wide : (i + 1) * wide].reshape(rows, wide),
            grads[...].reshape(rows, NARROW),
            (((0,), (0,)), ((), ())),
            preferred_element_type=F32,
        ).reshape(8, 32, NARROW)
        b, core = i // 2, i % 2

        @pl.when(first_core == (core == 0))
        def _():
            for j in range(8):
                keep_ref[place(b, j)] = part[j]

        @pl.when(first_core != (core == 0))
        def _():
            for j in range(8):
                send_ref[place(b, j)] = part[j].astype(BF16)


def weight_call(pieces, grads):
    vmem = pl.BlockSpec(memory_space=pltpu.VMEM)
    return pl.pallas_call(
        weight_kernel,
        out_shape=[jax.ShapeDtypeStruct((16, 32, NARROW), kind) for kind in (F32, BF16)]
        + [jax.ShapeDtypeStruct((MEMBERS, LIVE, NARROW), BF16)],
        in_specs=[vmem] * 9,
        out_specs=[vmem] * 3,
        compiler_params=params(24 * 2**20),
        cost_estimate=pl.CostEstimate(
            flops=2 * MEMBERS * LIVE * CHUNK * NARROW, bytes_accessed=5 * 2**20, transcendentals=0
        ),
        name="weight_part",
    )(pieces, *grads)


def project_kernel(w_ref, s_ref, grads, *refs):
    out_refs, (top_ref, held) = refs[:MEMBERS], refs[MEMBERS:]
    rows = MEMBERS * LIVE
    wide = 256
    proj = jnp.dot(s_ref[...].reshape(rows, CHUNK), w_ref[...], preferred_element_type=F32)
    held[:, :, :NARROW] = proj.astype(BF16).reshape(MEMBERS, LIVE, NARROW)
    top = jnp.zeros((8, wide), F32)
    for i in range(CHUNK // wide):
        part = lax.dot_general(
            grads[...].reshape(rows, NARROW),
            w_ref[i * wide : (i + 1) * wide, :],
            (((1,), (1,)), ((), ())),
            preferred_element_type=F32,
        )
        held[:, :, NARROW + i * wide : NARROW + (i + 1) * wide] = part.astype(BF16).reshape(
            MEMBERS, LIVE, wide
        )
        top = jnp.maximum(top, jnp.max(jnp.abs(part).reshape(rows // 8, 8, wide), axis=0))
    for out_ref, f in zip(out_refs, rows_at(1)):
        out_ref[...] = held[f]
    top_ref[...] = jnp.broadcast_to(jnp.max(top), (1, 128))


def project_call(weights, pieces, grads):
    vmem = pl.BlockSpec(memory_space=pltpu.VMEM)
    out = pl.pallas_call(
        project_kernel,
        out_shape=[pltpu.VMEM((LIVE, BOTH), BF16)]
        + [pltpu.HBM((LIVE, BOTH), BF16)] * (MEMBERS - 1)
        + [jax.ShapeDtypeStruct((1, 128), F32)],
        in_specs=[vmem] * 3,
        out_specs=[vmem] * 9,
        scratch_shapes=[
            pltpu.VMEM((MEMBERS, LIVE, BOTH), BF16),
        ],
        compiler_params=params(24 * 2**20),
        cost_estimate=pl.CostEstimate(
            flops=4 * MEMBERS * LIVE * CHUNK * NARROW, bytes_accessed=6 * 2**20, transcendentals=0
        ),
        name="project",
    )(weights, pieces, grads)
    return out[:MEMBERS], out[MEMBERS]


def peak_kernel(parts_ref, top_ref, sum_ref, tops_ref):
    total = parts_ref[0].astype(F32)
    for i in range(1, 16):
        total = total + parts_ref[i].astype(F32)
    sum_ref[...] = total
    lane = lax.broadcasted_iota(jnp.int32, (1, 128), 1)
    both = jnp.where(lane < 64, top_ref[...], jnp.max(jnp.abs(total)))
    tops_ref[...] = jnp.broadcast_to(both[None], (256, 1, 128))


def peak_call(parts, top):
    vmem = pl.BlockSpec(memory_space=pltpu.VMEM)
    return pl.pallas_call(
        peak_kernel,
        out_shape=[
            jax.ShapeDtypeStruct((32, NARROW), F32),
            jax.ShapeDtypeStruct((256, 1, 128), F32),
        ],
        in_specs=[vmem, vmem],
        out_specs=[vmem, vmem],
        compiler_params=params(16 * 2**20),
        cost_estimate=pl.CostEstimate(flops=16 * 32 * NARROW, bytes_accessed=2**20, transcendentals=0),
        name="peaks",
    )(parts, top)


def finish_kernel(tops_ref, sum_ref, *refs):
    back_refs, (input_ref, weight_ref, held, sems) = refs[:MEMBERS], refs[MEMBERS:]
    tops = jnp.max(tops_ref[...], axis=0)
    scale = 1.0 / (tops[:, :1] + peak_eps)
    held[:, LIVE:, :] = jnp.zeros((MEMBERS, ROWS - LIVE, CHUNK), BF16)
    copies = []
    for i, (ref, f) in enumerate(zip(back_refs, rows_at(-1))):
        held[i, :LIVE] = (ref[:, NARROW:].astype(F32) * scale).astype(BF16)
        columns = pl.ds(pl.multiple_of(f * CHUNK, CHUNK), CHUNK)
        copies.append(pltpu.make_async_copy(held.at[i], input_ref.at[:, columns], sems.at[i]))
        copies[-1].start()
    weight_ref[...] = sum_ref[...] / (tops[:, 64:65] + peak_eps)
    for copy in copies:
        copy.wait()


def finish_call(tops, both, weight_sum):
    vmem = pl.BlockSpec(memory_space=pltpu.VMEM)
    return pl.pallas_call(
        finish_kernel,
        out_shape=[
            jax.ShapeDtypeStruct((ROWS, D), BF16),
            jax.ShapeDtypeStruct((32, NARROW), F32),
        ],
        in_specs=[vmem] * (2 + MEMBERS),
        out_specs=[pl.BlockSpec(memory_space=pl.ANY), vmem],
        scratch_shapes=[
            pltpu.VMEM((MEMBERS, ROWS, CHUNK), BF16),
            pltpu.SemaphoreType.DMA((MEMBERS,)),
        ],
        compiler_params=params(16 * 2**20),
        cost_estimate=pl.CostEstimate(flops=LIVE * D, bytes_accessed=4 * ROWS * D, transcendentals=0),
        name="finish",
    )(tops, weight_sum, *both)


def shards(
    section_input,
    c_weight,
    scan_input,
    b_factors,
    step_size,
    decay_rate,
    skip_gain,
    out_grad,
    doc_index,
    kept_rows,
    send_counts,
):
    kept = kept_rows.reshape(1, 32)
    sends = send_counts.reshape(32, 32)
    rate, docs = decay_rate.reshape(1, HEADS), doc_index.reshape(1, ROWS)

    pieces = exchange(pack(section_input), WIDE)

    c_own = c_grad_call(kept, sends, rate, docs, step_size, out_grad, scan_input, b_factors)
    grads = [c_own] + [lax.ppermute(c_own, ALL, moved(*step)) for step in STEPS[1:]]

    keep, send, grads = weight_call(pieces, grads)
    both, top = project_call(c_weight, pieces, grads)
    got = to_core(send)
    got, top = lax.optimization_barrier((got, top))
    parts = (keep + got.astype(F32)).astype(BF16)
    parts = lax.all_to_all(parts, "dp", 0, 0, axis_index_groups=SAME_CORE)

    both = [both[0]] + [lax.ppermute(value, ALL, moved(*step)) for value, step in zip(both[1:], STEPS[1:])]
    weight_sum, tops = peak_call(parts, top)
    tops = exchange(tops, None)
    weight_sum = lax.ppermute(weight_sum, ALL, HOME)
    both = [pltpu.with_memory_space_constraint(value, pltpu.VMEM) for value in both]
    scan_grad = scan_grad_call(
        kept, sends, skip_gain, rate, docs, step_size, out_grad, b_factors, both
    )
    input_grad, readout_weight_gradient = finish_call(tops, both, weight_sum)
    return (input_grad, scan_grad, readout_weight_gradient)


def solution(mesh):
    rows = P(ALL, None)
    placed = (
        rows,
        P("fsdp", None),
        rows,
        rows,
        P(None, ALL),
        P(),
        P(),
        rows,
        P(ALL),
        P(None, "fsdp"),
        P(None, "fsdp", None),
    )
    return jax.shard_map(
        shards, mesh=mesh, in_specs=placed, out_specs=(rows, rows, rows), check_vma=False
    )
```

```python
import jax
import jax.numpy as jnp
from jax import lax
from jax.experimental import pallas as pl
from jax.experimental.pallas import tpu as pltpu
from jax.sharding import PartitionSpec as P

GROUPS = 4
STATE = 128
HEADS = 128
HDIM = 64
HPG = HEADS // GROUPS
ROWS = 128
LIVE = 96
D = 8192
NARROW = GROUPS * STATE
MEMBERS = 8
CHUNK = D // MEMBERS
BOTH = NARROW + CHUNK
VMEM_LIMIT = 60 * 2**20
LOG2E = 1.4426950408889634
ALL = ("dp", "fsdp")
peak_eps = 1e-06
F32 = jnp.float32
BF16 = jnp.bfloat16


def joint(y_hi, x, y_lo, z, core):
    return (y_lo * 16 + z * 2 + core) * 8 + y_hi * 4 + x


WIDE = [
    [joint(h, x, h ^ s, z, c) for h in (0, 1) for x in range(4)]
    for s in (0, 1)
    for z in range(8)
    for c in (0, 1)
]
def moved(dx, pair):
    return [
        (joint(h, x, l, z, c), joint(h ^ pair, (x + dx) % 4, l ^ pair, z, c))
        for h in (0, 1)
        for x in range(4)
        for l in (0, 1)
        for z in range(8)
        for c in (0, 1)
    ]


STEPS = [(0, 0), (2, 1), (2, 0), (1, 1), (3, 1), (0, 1), (1, 0), (3, 0)]
CORE_SWAP = [(i, i ^ 1) for i in range(32)]
SAME_CORE = [[l * 16 + z * 2 + c for l in (0, 1) for z in range(8)] for c in (0, 1)]
AWAY = (3, 2, 0, 1)


def summed_at(x, b, x_home):
    away = AWAY[(x_home - x) % 4]
    return (2 * x + 1 + away) % 8 if b else (2 * x - away) % 8


HOME = [
    (joint(h, x, k, summed_at(x, b, i), c), joint(k, i, h, 2 * x + b, c))
    for h in (0, 1)
    for x in range(4)
    for k in (0, 1)
    for i in range(4)
    for b in (0, 1)
    for c in (0, 1)
]


def exchange(value, groups):
    return lax.all_to_all(value, ALL, 0, 0, axis_index_groups=groups)


def to_core(value):
    return lax.ppermute(value, "dp", CORE_SWAP)


def coordinates():
    dp, f = lax.axis_index("dp"), lax.axis_index("fsdp")
    return dict(dp=dp, core=dp % 2, y_lo=dp // 16, x=f % 4, y_hi=f // 4)


def rows_at(sign):
    at = coordinates()
    return [(at["y_hi"] + pair) % 2 * 4 + (at["x"] + 4 + sign * dx) % 4 for dx, pair in STEPS]


def params(limit=VMEM_LIMIT):
    return pltpu.CompilerParams(vmem_limit_bytes=limit)


def pack_kernel(s_ref, wide_ref, sems):
    copies = [
        pltpu.make_async_copy(
            s_ref.at[pl.ds(0, LIVE), pl.ds(f * CHUNK, CHUNK)], wide_ref.at[f], sems.at[f]
        )
        for f in range(MEMBERS)
    ]
    for copy in copies:
        copy.start()
    for copy in copies:
        copy.wait()


def pack(section_input):
    return pl.pallas_call(
        pack_kernel,
        out_shape=jax.ShapeDtypeStruct((MEMBERS, LIVE, CHUNK), BF16),
        in_specs=[pl.BlockSpec(memory_space=pl.ANY)],
        out_specs=pl.BlockSpec(memory_space=pltpu.VMEM),
        scratch_shapes=[pltpu.SemaphoreType.DMA((MEMBERS,))],
        compiler_params=params(),
        cost_estimate=pl.CostEstimate(flops=0, bytes_accessed=4 * LIVE * D, transcendentals=0),
        name="pack",
    )(section_input)


def live_count(kept_ref, sends_ref):
    dp = coordinates()["dp"]
    row, column = (lax.broadcasted_iota(jnp.int32, (32, 32), k) for k in range(2))
    counts = jnp.where(row == dp, sends_ref[...], 0) + jnp.where(
        (row == 0) & (column == dp), kept_ref[...], 0
    )
    counts = jnp.sum(counts.astype(F32), axis=0, keepdims=True)
    return jnp.sum(counts, axis=1, keepdims=True)


def places(shape):
    rows = [lax.broadcasted_iota(jnp.int32, shape, k).astype(F32) for k in range(2)]
    return rows


def head_tables(rate_ref, step_ref):
    steps = step_ref[...]
    totals = steps * jnp.transpose(jnp.broadcast_to(rate_ref[...], (HEADS, HEADS)))
    lane = lax.broadcasted_iota(jnp.int32, totals.shape, 1)
    reach = 1
    while reach < ROWS:
        totals = totals + jnp.where(lane >= reach, pltpu.roll(totals, reach, 1), 0.0)
        reach *= 2
    totals = totals * LOG2E
    return totals, totals + jnp.log(steps) * LOG2E


def keep_tables(along_ref, down_ref, along, down):
    along_ref[...] = along
    down = jnp.transpose(down)
    for q in range(GROUPS):
        down_ref[q] = pltpu.roll(down, HEADS - q * HPG, 1) if q else down


def row_mask(live, doc_ref, target, source):
    along = jnp.broadcast_to(doc_ref[...].astype(F32), (ROWS, ROWS))
    down = jnp.transpose(along)
    keep = (along[:LIVE] == down[:LIVE]) & (source <= target) & (target < live) & (source < live)
    return jnp.where(keep, 0.0, -1e30).astype(F32)


def group_rows(q):
    return pl.ds(pl.multiple_of(q * HPG, HPG), HPG)


def c_grad_kernel(
    kept_ref, sends_ref, rate_ref, doc_ref, step_ref, g_ref, x_ref, b_ref, out_ref, source_scr, totals_scr, bias_scr
):
    q = pl.program_id(0)

    @pl.when(q == 0)
    def _():
        totals, source = head_tables(rate_ref, step_ref)
        keep_tables(source_scr, totals_scr, source, totals)
        t, s = places((LIVE, ROWS))
        bias_scr[...] = row_mask(live_count(kept_ref, sends_ref), doc_ref, t, s)

    bias = bias_scr[...]
    source = source_scr[group_rows(q), :]
    totals_col = totals_scr[q]
    upper = lax.broadcasted_iota(jnp.int32, (128, ROWS), 0) < HDIM
    mixing = jnp.zeros((LIVE, ROWS), F32)
    for p in range(HPG // 2):
        lanes = slice(p * 128, p * 128 + 128)
        x_pair = x_ref[:, lanes]
        zero = jnp.zeros_like(x_pair)
        x_turned = jnp.transpose(x_pair)
        both = jnp.concatenate([jnp.where(upper, x_turned, zero), jnp.where(upper, zero, x_turned)], axis=1)
        inner = jnp.dot(g_ref[:, lanes], both, preferred_element_type=F32)
        for k in range(2):
            h = 2 * p + k
            gap = (source[h : h + 1, :] - totals_col[:LIVE, h : h + 1]) + bias
            mixing = mixing + jnp.exp2(gap) * inner[:, k * 128 : k * 128 + 128]
    c_grad = jnp.dot(mixing.astype(BF16), b_ref[...], preferred_element_type=F32).astype(BF16)
    out_ref[...] = c_grad


def smem():
    return pl.BlockSpec(memory_space=pltpu.SMEM)


def row_spec():
    return pl.BlockSpec((1, 128), lambda q: (0, 0))


def c_grad_call(kept, sends, rate, docs, steps, out_grad, scan_input, b_factors):
    wide = HPG * HDIM
    return pl.pallas_call(
        c_grad_kernel,
        grid=(GROUPS,),
        out_shape=pltpu.VMEM((LIVE, NARROW), BF16),
        in_specs=[
            pl.BlockSpec((1, 32), lambda q: (0, 0)),
            pl.BlockSpec((32, 32), lambda q: (0, 0)),
            row_spec(),
            row_spec(),
            pl.BlockSpec((HEADS, ROWS), lambda q: (0, 0)),
            pl.BlockSpec((LIVE, wide), lambda q: (0, q)),
            pl.BlockSpec((ROWS, wide), lambda q: (0, q)),
            pl.BlockSpec((ROWS, STATE), lambda q: (0, q)),
        ],
        out_specs=pl.BlockSpec((LIVE, STATE), lambda q: (0, q)),
        scratch_shapes=[
            pltpu.VMEM((HEADS, ROWS), F32),
            pltpu.VMEM((GROUPS, ROWS, HEADS), F32),
            pltpu.VMEM((LIVE, ROWS), F32),
        ],
        compiler_params=params(),
        cost_estimate=pl.CostEstimate(
            flops=4 * LIVE * ROWS * D, bytes_accessed=4 * ROWS * D, transcendentals=HEADS * LIVE * ROWS
        ),
        name="c_grad",
    )(kept, sends, rate, docs, steps, out_grad, scan_input, b_factors)


def tables_kernel(kept_ref, sends_ref, rate_ref, doc_ref, step_ref, out_ref):
    totals, source = head_tables(rate_ref, step_ref)
    out_ref[0] = totals
    out_ref[1] = jnp.transpose(source)
    s, t = places((LIVE, ROWS))
    live = live_count(kept_ref, sends_ref)
    out_ref[2, :LIVE] = row_mask(live, doc_ref, t, s)
    out_ref[2, LIVE:] = jnp.zeros((ROWS - LIVE, ROWS), F32)
    out_ref[3, :LIVE] = jnp.where(s < live, 1.0, 0.0)
    out_ref[3, LIVE:] = jnp.zeros((ROWS - LIVE, ROWS), F32)


def tables_call(kept, sends, rate, docs, steps):
    vmem = pl.BlockSpec(memory_space=pltpu.VMEM)
    return pl.pallas_call(
        tables_kernel,
        out_shape=pltpu.HBM((4, ROWS, ROWS), F32),
        in_specs=[vmem] * 5,
        out_specs=vmem,
        compiler_params=params(),
        cost_estimate=pl.CostEstimate(flops=0, bytes_accessed=2**19, transcendentals=HEADS * ROWS),
        name="tables",
    )(kept, sends, rate, docs, steps)


def scan_grad_kernel(skip_ref, tables_ref, g_ref, b_ref, *refs):
    q = pl.program_id(0)
    proj_refs, (out_ref, source_scr) = refs[:MEMBERS], refs[MEMBERS:]

    @pl.when(q == 0)
    def _():
        source = tables_ref[1]
        for k in range(GROUPS):
            source_scr[k] = pltpu.roll(source, HEADS - k * HPG, 1) if k else source

    bias = tables_ref[2, :LIVE, :]
    alive = tables_ref[3, :LIVE, :]
    totals = tables_ref[0, group_rows(q), :]
    source_col = source_scr[q]
    half = lax.broadcasted_iota(jnp.int32, (ROWS, 128), 1) < HDIM
    c_proj = proj_refs[0][...].astype(F32)
    for proj_ref in proj_refs[1:]:
        c_proj = c_proj + proj_ref[...].astype(F32)
    c_proj = jnp.concatenate([c_proj.astype(BF16), jnp.zeros((ROWS - LIVE, STATE), BF16)], axis=0)
    affinity = lax.dot_general(
        b_ref[:LIVE, :], c_proj, (((1,), (1,)), ((), ())), preferred_element_type=F32
    )
    for p in range(HPG // 2):
        lanes = slice(p * 128, p * 128 + 128)
        g_pair = g_ref[:, lanes]
        zero = jnp.zeros_like(g_pair)
        both = jnp.concatenate([jnp.where(half, g_pair, zero), jnp.where(half, zero, g_pair)], axis=0)
        kernels = []
        for k in range(2):
            h = 2 * p + k
            gap = (source_col[:LIVE, h : h + 1] - totals[h : h + 1, :]) + bias
            kernels.append((jnp.exp2(gap) * affinity).astype(BF16))
        grads = jnp.dot(jnp.concatenate(kernels, axis=1), both, preferred_element_type=F32)
        first = q * HPG + 2 * p
        gain = jnp.where(half[:LIVE], skip_ref[first], skip_ref[first + 1]) * alive
        grads = grads + gain * g_pair[:LIVE].astype(F32)
        out_ref[:LIVE, lanes] = grads.astype(BF16)
    out_ref[LIVE:, :] = jnp.zeros((ROWS - LIVE, HPG * HDIM), BF16)


def scan_grad_call(skip, tables, out_grad, b_factors, shares):
    wide = HPG * HDIM
    return pl.pallas_call(
        scan_grad_kernel,
        grid=(GROUPS,),
        out_shape=jax.ShapeDtypeStruct((ROWS, D), BF16),
        in_specs=[
            smem(),
            pl.BlockSpec((4, ROWS, ROWS), lambda q: (0, 0, 0)),
            pl.BlockSpec((ROWS, wide), lambda q: (0, q)),
            pl.BlockSpec((ROWS, STATE), lambda q: (0, q)),
        ]
        + [pl.BlockSpec((LIVE, STATE), lambda q: (0, q))] * MEMBERS,
        out_specs=pl.BlockSpec((ROWS, wide), lambda q: (0, q)),
        scratch_shapes=[pltpu.VMEM((GROUPS, ROWS, HEADS), F32)],
        compiler_params=params(),
        cost_estimate=pl.CostEstimate(
            flops=4 * LIVE * ROWS * D, bytes_accessed=4 * ROWS * D, transcendentals=HEADS * LIVE * ROWS
        ),
        name="scan_grad",
    )(skip, tables, out_grad, b_factors, *shares)


def weight_kernel(s_ref, *refs):
    c_refs, (keep_ref, send_ref, grads) = refs[:MEMBERS], refs[MEMBERS:]
    for c_ref, f in zip(c_refs, rows_at(-1)):
        grads[f] = c_ref[...]
    at = coordinates()
    first_core = at["core"] == 0

    def place(b, j):
        step = (j % 4 + 4 - at["x"]) % 4
        away = jnp.where(step == 0, AWAY[0], jnp.where(step == 1, AWAY[1], jnp.where(step == 2, AWAY[2], AWAY[3])))
        z = 2 * at["x"] + 1 + away if b else 2 * at["x"] + 8 - away
        return j // 4 * 8 + z % 8

    wide = 256
    rows = MEMBERS * LIVE
    for i in range(CHUNK // wide):
        part = lax.dot_general(
            s_ref[:, :, i * wide : (i + 1) * wide].reshape(rows, wide),
            grads[...].reshape(rows, NARROW),
            (((0,), (0,)), ((), ())),
            preferred_element_type=F32,
        ).reshape(8, 32, NARROW)
        b, core = i // 2, i % 2

        @pl.when(first_core == (core == 0))
        def _():
            for j in range(8):
                keep_ref[place(b, j)] = part[j]

        @pl.when(first_core != (core == 0))
        def _():
            for j in range(8):
                send_ref[place(b, j)] = part[j].astype(BF16)


def weight_call(pieces, grads):
    vmem = pl.BlockSpec(memory_space=pltpu.VMEM)
    return pl.pallas_call(
        weight_kernel,
        out_shape=[jax.ShapeDtypeStruct((16, 32, NARROW), kind) for kind in (F32, BF16)]
        + [jax.ShapeDtypeStruct((MEMBERS, LIVE, NARROW), BF16)],
        in_specs=[vmem] * 9,
        out_specs=[vmem] * 3,
        compiler_params=params(24 * 2**20),
        cost_estimate=pl.CostEstimate(
            flops=2 * MEMBERS * LIVE * CHUNK * NARROW, bytes_accessed=5 * 2**20, transcendentals=0
        ),
        name="weight_part",
    )(pieces, *grads)


def c_proj_kernel(w_ref, s_ref, out_ref):
    rows = MEMBERS * LIVE
    part = jnp.dot(s_ref[...].reshape(rows, CHUNK), w_ref[...], preferred_element_type=F32)
    out_ref[...] = part.astype(BF16).reshape(MEMBERS, LIVE, NARROW)


def c_proj_call(weights, pieces):
    vmem = pl.BlockSpec(memory_space=pltpu.VMEM)
    return pl.pallas_call(
        c_proj_kernel,
        out_shape=jax.ShapeDtypeStruct((MEMBERS, LIVE, NARROW), BF16),
        in_specs=[vmem] * 2,
        out_specs=vmem,
        compiler_params=params(24 * 2**20),
        cost_estimate=pl.CostEstimate(
            flops=2 * MEMBERS * LIVE * CHUNK * NARROW, bytes_accessed=4 * 2**20, transcendentals=0
        ),
        name="c_proj",
    )(weights, pieces)


def project_kernel(w_ref, proj_ref, grads, *refs):
    out_refs, (top_ref, held, sems) = refs[:MEMBERS], refs[MEMBERS:]
    rows = MEMBERS * LIVE
    wide = 256
    dests = rows_at(1)
    copies = []
    for k, (first, last) in enumerate(((0, NARROW + CHUNK // 2), (NARROW + CHUNK // 2, BOTH))):
        columns = pl.ds(first, last - first)
        copies.append(
            [
                pltpu.make_async_copy(held.at[f, :, columns], ref.at[:, columns], sems.at[k, i])
                for i, (ref, f) in enumerate(zip(out_refs, dests))
            ]
        )
    held[:, :, :NARROW] = proj_ref[...]
    top = jnp.zeros((8, wide), F32)
    steps = CHUNK // wide
    for i in range(steps):
        part = lax.dot_general(
            grads[...].reshape(rows, NARROW),
            w_ref[i * wide : (i + 1) * wide, :],
            (((1,), (1,)), ((), ())),
            preferred_element_type=F32,
        )
        held[:, :, NARROW + i * wide : NARROW + (i + 1) * wide] = part.astype(BF16).reshape(
            MEMBERS, LIVE, wide
        )
        top = jnp.maximum(top, jnp.max(jnp.abs(part).reshape(rows // 8, 8, wide), axis=0))
        if i % (steps // 2) == steps // 2 - 1:
            for copy in copies[i // (steps // 2)]:
                copy.start()
    top_ref[...] = jnp.broadcast_to(jnp.max(top), (1, 128))
    for copy in copies[0] + copies[1]:
        copy.wait()


def project_call(weights, proj, grads):
    vmem = pl.BlockSpec(memory_space=pltpu.VMEM)
    out = pl.pallas_call(
        project_kernel,
        out_shape=[pltpu.VMEM((LIVE, BOTH), BF16)]
        + [pltpu.HBM((LIVE, BOTH), BF16)] * (MEMBERS - 1)
        + [jax.ShapeDtypeStruct((1, 128), F32)],
        in_specs=[vmem] * 3,
        out_specs=[pl.BlockSpec(memory_space=pl.ANY)] * MEMBERS + [vmem],
        scratch_shapes=[
            pltpu.VMEM((MEMBERS, LIVE, BOTH), BF16),
            pltpu.SemaphoreType.DMA((2, MEMBERS)),
        ],
        compiler_params=params(24 * 2**20),
        cost_estimate=pl.CostEstimate(
            flops=2 * MEMBERS * LIVE * CHUNK * NARROW, bytes_accessed=6 * 2**20, transcendentals=0
        ),
        name="project",
    )(weights, proj, grads)
    return out[:MEMBERS], out[MEMBERS]


def peak_kernel(parts_ref, top_ref, sum_ref, tops_ref):
    total = parts_ref[0].astype(F32)
    for i in range(1, 16):
        total = total + parts_ref[i].astype(F32)
    sum_ref[...] = total
    lane = lax.broadcasted_iota(jnp.int32, (1, 128), 1)
    both = jnp.where(lane < 64, top_ref[...], jnp.max(jnp.abs(total)))
    tops_ref[...] = jnp.broadcast_to(both[None], (256, 1, 128))


def peak_call(parts, top):
    vmem = pl.BlockSpec(memory_space=pltpu.VMEM)
    return pl.pallas_call(
        peak_kernel,
        out_shape=[
            jax.ShapeDtypeStruct((32, NARROW), F32),
            jax.ShapeDtypeStruct((256, 1, 128), F32),
        ],
        in_specs=[vmem, vmem],
        out_specs=[vmem, vmem],
        compiler_params=params(16 * 2**20),
        cost_estimate=pl.CostEstimate(flops=16 * 32 * NARROW, bytes_accessed=2**20, transcendentals=0),
        name="peaks",
    )(parts, top)


def finish_kernel(tops_ref, sum_ref, *refs):
    back_refs, (input_ref, weight_ref, held, sems) = refs[:MEMBERS], refs[MEMBERS:]
    tops = jnp.max(tops_ref[...], axis=0)
    scale = 1.0 / (tops[:, :1] + peak_eps)
    held[:, LIVE:, :] = jnp.zeros((MEMBERS, ROWS - LIVE, CHUNK), BF16)
    copies = []
    for i, (ref, f) in enumerate(zip(back_refs, rows_at(-1))):
        held[i, :LIVE] = (ref[:, NARROW:].astype(F32) * scale).astype(BF16)
        columns = pl.ds(pl.multiple_of(f * CHUNK, CHUNK), CHUNK)
        copies.append(pltpu.make_async_copy(held.at[i], input_ref.at[:, columns], sems.at[i]))
        copies[-1].start()
    weight_ref[...] = sum_ref[...] / (tops[:, 64:65] + peak_eps)
    for copy in copies:
        copy.wait()


def finish_call(tops, both, weight_sum):
    vmem = pl.BlockSpec(memory_space=pltpu.VMEM)
    return pl.pallas_call(
        finish_kernel,
        out_shape=[
            jax.ShapeDtypeStruct((ROWS, D), BF16),
            jax.ShapeDtypeStruct((32, NARROW), F32),
        ],
        in_specs=[vmem] * (2 + MEMBERS),
        out_specs=[pl.BlockSpec(memory_space=pl.ANY), vmem],
        scratch_shapes=[
            pltpu.VMEM((MEMBERS, ROWS, CHUNK), BF16),
            pltpu.SemaphoreType.DMA((MEMBERS,)),
        ],
        compiler_params=params(16 * 2**20),
        cost_estimate=pl.CostEstimate(flops=LIVE * D, bytes_accessed=4 * ROWS * D, transcendentals=0),
        name="finish",
    )(tops, weight_sum, *both)


def shards(
    section_input,
    c_weight,
    scan_input,
    b_factors,
    step_size,
    decay_rate,
    skip_gain,
    out_grad,
    doc_index,
    kept_rows,
    send_counts,
):
    kept = kept_rows.reshape(1, 32)
    sends = send_counts.reshape(32, 32)
    rate, docs = decay_rate.reshape(1, HEADS), doc_index.reshape(1, ROWS)

    pieces = exchange(pack(section_input), WIDE)

    c_own = c_grad_call(kept, sends, rate, docs, step_size, out_grad, scan_input, b_factors)
    grads = [c_own] + [lax.ppermute(c_own, ALL, moved(*step)) for step in STEPS[1:]]

    steps, c_own = lax.optimization_barrier((step_size, c_own))
    tables = tables_call(kept, sends, rate, docs, steps)
    proj = c_proj_call(c_weight, pieces)
    grads, tables, proj = lax.optimization_barrier((grads, tables, proj))
    keep, send, grads = weight_call(pieces, grads)
    both, top = project_call(c_weight, proj, grads)
    got = to_core(send)
    got, top = lax.optimization_barrier((got, top))
    parts = (keep + got.astype(F32)).astype(BF16)
    parts = lax.all_to_all(parts, "dp", 0, 0, axis_index_groups=SAME_CORE)

    back = [both[0]] + [lax.ppermute(both[i], ALL, moved(*STEPS[i])) for i in range(1, 7)]
    weight_sum, tops = peak_call(parts, top)
    weight_sum, *late = lax.optimization_barrier((weight_sum, *both[7:]))
    tops = exchange(tops, None)
    back += [lax.ppermute(value, ALL, moved(*step)) for value, step in zip(late, STEPS[7:])]
    weight_sum = lax.ppermute(weight_sum, ALL, HOME)
    both = [pltpu.with_memory_space_constraint(value, pltpu.VMEM) for value in back]
    scan_grad = scan_grad_call(skip_gain, tables, out_grad, b_factors, both)
    input_grad, readout_weight_gradient = finish_call(tops, both, weight_sum)
    return (input_grad, scan_grad, readout_weight_gradient)


def solution(mesh):
    rows = P(ALL, None)
    placed = (
        rows,
        P("fsdp", None),
        rows,
        rows,
        P(None, ALL),
        P(),
        P(),
        rows,
        P(ALL),
        P(None, "fsdp"),
        P(None, "fsdp", None),
    )
    return jax.shard_map(
        shards, mesh=mesh, in_specs=placed, out_specs=(rows, rows, rows), check_vma=False
    )
```

```python
import jax
import jax.numpy as jnp
from jax import lax
from jax.experimental import pallas as pl
from jax.experimental.pallas import tpu as pltpu
from jax.sharding import PartitionSpec as P

GROUPS = 4
STATE = 128
HEADS = 128
HDIM = 64
HPG = HEADS // GROUPS
ROWS = 128
LIVE = 96
D = 8192
NARROW = GROUPS * STATE
MEMBERS = 8
CHUNK = D // MEMBERS
BOTH = NARROW + CHUNK
HALF = BOTH // 2
VMEM_LIMIT = 60 * 2**20
C_STEP = 4
SCAN_STEP = 2
LOG2E = 1.4426950408889634
ALL = ("dp", "fsdp")
peak_eps = 1e-06
F32 = jnp.float32
BF16 = jnp.bfloat16


def joint(y_hi, x, y_lo, z, core):
    return (y_lo * 16 + z * 2 + core) * 8 + y_hi * 4 + x


WIDE = [
    [joint(h, x, h ^ s, z, c) for h in (0, 1) for x in range(4)]
    for s in (0, 1)
    for z in range(8)
    for c in (0, 1)
]
def moved(dx, pair):
    return [
        (joint(h, x, l, z, c), joint(h ^ pair, (x + dx) % 4, l ^ pair, z, c))
        for h in (0, 1)
        for x in range(4)
        for l in (0, 1)
        for z in range(8)
        for c in (0, 1)
    ]


STEPS = [(0, 0), (2, 1), (2, 0), (1, 1), (3, 1), (0, 1), (1, 0), (3, 0)]
CORE_SWAP = [(i, i ^ 1) for i in range(32)]
SAME_CORE = [[l * 16 + z * 2 + c for l in (0, 1) for z in range(8)] for c in (0, 1)]
AWAY = (3, 2, 0, 1)


def summed_at(x, b, x_home):
    away = AWAY[(x_home - x) % 4]
    return (2 * x + 1 + away) % 8 if b else (2 * x - away) % 8


HOME = [
    (joint(h, x, k, summed_at(x, b, i), c), joint(k, i, h, 2 * x + b, c))
    for h in (0, 1)
    for x in range(4)
    for k in (0, 1)
    for i in range(4)
    for b in (0, 1)
    for c in (0, 1)
]


def exchange(value, groups):
    return lax.all_to_all(value, ALL, 0, 0, axis_index_groups=groups)


def to_core(value):
    return lax.ppermute(value, "dp", CORE_SWAP)


def coordinates():
    dp, f = lax.axis_index("dp"), lax.axis_index("fsdp")
    return dict(dp=dp, core=dp % 2, y_lo=dp // 16, x=f % 4, y_hi=f // 4)


def rows_at(sign):
    at = coordinates()
    return [(at["y_hi"] + pair) % 2 * 4 + (at["x"] + 4 + sign * dx) % 4 for dx, pair in STEPS]


def params(limit=VMEM_LIMIT):
    return pltpu.CompilerParams(vmem_limit_bytes=limit)


def pack_kernel(s_ref, wide_ref, sems):
    copies = [
        pltpu.make_async_copy(
            s_ref.at[pl.ds(0, LIVE), pl.ds(f * CHUNK, CHUNK)], wide_ref.at[f], sems.at[f]
        )
        for f in range(MEMBERS)
    ]
    for copy in copies:
        copy.start()
    for copy in copies:
        copy.wait()


def pack(section_input):
    return pl.pallas_call(
        pack_kernel,
        out_shape=jax.ShapeDtypeStruct((MEMBERS, LIVE, CHUNK), BF16),
        in_specs=[pl.BlockSpec(memory_space=pl.ANY)],
        out_specs=pl.BlockSpec(memory_space=pltpu.VMEM),
        scratch_shapes=[pltpu.SemaphoreType.DMA((MEMBERS,))],
        compiler_params=params(),
        cost_estimate=pl.CostEstimate(flops=0, bytes_accessed=4 * LIVE * D, transcendentals=0),
        name="pack",
    )(section_input)


def live_count(kept_ref, sends_ref):
    dp = coordinates()["dp"]
    row, column = (lax.broadcasted_iota(jnp.int32, (32, 32), k) for k in range(2))
    counts = jnp.where(row == dp, sends_ref[...], 0) + jnp.where(
        (row == 0) & (column == dp), kept_ref[...], 0
    )
    counts = jnp.sum(counts.astype(F32), axis=0, keepdims=True)
    return jnp.sum(counts, axis=1, keepdims=True)


def places(shape):
    rows = [lax.broadcasted_iota(jnp.int32, shape, k).astype(F32) for k in range(2)]
    return rows


def head_tables(rate_ref, step_ref):
    steps = step_ref[...]
    totals = steps * jnp.transpose(jnp.broadcast_to(rate_ref[...], (HEADS, HEADS)))
    lane = lax.broadcasted_iota(jnp.int32, totals.shape, 1)
    reach = 1
    while reach < ROWS:
        totals = totals + jnp.where(lane >= reach, pltpu.roll(totals, reach, 1), 0.0)
        reach *= 2
    totals = totals * LOG2E
    return totals, totals + jnp.log(steps) * LOG2E


def keep_tables(along_ref, down_ref, along, down):
    along_ref[...] = along
    down = jnp.transpose(down)
    for q in range(GROUPS):
        down_ref[q] = pltpu.roll(down, HEADS - q * HPG, 1) if q else down


def row_mask(live, doc_ref, target, source):
    along = jnp.broadcast_to(doc_ref[...].astype(F32), (ROWS, ROWS))
    down = jnp.transpose(along)
    keep = (along[:LIVE] == down[:LIVE]) & (source <= target) & (target < live) & (source < live)
    return jnp.where(keep, 0.0, -1e30).astype(F32)


def group_rows(q):
    return pl.ds(pl.multiple_of(q * HPG, HPG), HPG)


def c_grad_kernel(
    kept_ref, sends_ref, rate_ref, doc_ref, step_ref, g_ref, x_ref, b_ref, out_ref, source_scr, totals_scr, bias_scr
):
    step = pl.program_id(0)

    @pl.when(step == 0)
    def _():
        totals, source = head_tables(rate_ref, step_ref)
        keep_tables(source_scr, totals_scr, source, totals)
        t, s = places((LIVE, ROWS))
        bias_scr[...] = row_mask(live_count(kept_ref, sends_ref), doc_ref, t, s)

    bias = bias_scr[...]
    upper = lax.broadcasted_iota(jnp.int32, (128, ROWS), 0) < HDIM
    for k in range(C_STEP):
        q = step * C_STEP + k
        source = source_scr[group_rows(q), :]
        totals_col = totals_scr[q]
        mixing = jnp.zeros((LIVE, ROWS), F32)
        for p in range(HPG // 2):
            lanes = slice(k * HPG * HDIM + p * 128, k * HPG * HDIM + p * 128 + 128)
            x_pair = x_ref[:, lanes]
            zero = jnp.zeros_like(x_pair)
            x_turned = jnp.transpose(x_pair)
            both = jnp.concatenate([jnp.where(upper, x_turned, zero), jnp.where(upper, zero, x_turned)], axis=1)
            inner = jnp.dot(g_ref[:, lanes], both, preferred_element_type=F32)
            for i in range(2):
                h = 2 * p + i
                gap = (source[h : h + 1, :] - totals_col[:LIVE, h : h + 1]) + bias
                mixing = mixing + jnp.exp2(gap) * inner[:, i * 128 : i * 128 + 128]
        columns = slice(k * STATE, (k + 1) * STATE)
        out_ref[:, columns] = jnp.dot(
            mixing.astype(BF16), b_ref[:, columns], preferred_element_type=F32
        ).astype(BF16)


def smem():
    return pl.BlockSpec(memory_space=pltpu.SMEM)


def row_spec():
    return pl.BlockSpec((1, 128), lambda q: (0, 0))


def c_grad_call(kept, sends, rate, docs, steps, out_grad, scan_input, b_factors):
    wide, narrow = C_STEP * HPG * HDIM, C_STEP * STATE
    return pl.pallas_call(
        c_grad_kernel,
        grid=(GROUPS // C_STEP,),
        out_shape=pltpu.VMEM((LIVE, NARROW), BF16),
        in_specs=[
            pl.BlockSpec((1, 32), lambda q: (0, 0)),
            pl.BlockSpec((32, 32), lambda q: (0, 0)),
            row_spec(),
            row_spec(),
            pl.BlockSpec((HEADS, ROWS), lambda q: (0, 0)),
            pl.BlockSpec((LIVE, wide), lambda q: (0, q)),
            pl.BlockSpec((ROWS, wide), lambda q: (0, q)),
            pl.BlockSpec((ROWS, narrow), lambda q: (0, q)),
        ],
        out_specs=pl.BlockSpec((LIVE, narrow), lambda q: (0, q)),
        scratch_shapes=[
            pltpu.VMEM((HEADS, ROWS), F32),
            pltpu.VMEM((GROUPS, ROWS, HEADS), F32),
            pltpu.VMEM((LIVE, ROWS), F32),
        ],
        compiler_params=params(),
        cost_estimate=pl.CostEstimate(
            flops=4 * LIVE * ROWS * D, bytes_accessed=4 * ROWS * D, transcendentals=HEADS * LIVE * ROWS
        ),
        name="c_grad",
    )(kept, sends, rate, docs, steps, out_grad, scan_input, b_factors)


def tables_kernel(kept_ref, sends_ref, rate_ref, doc_ref, step_ref, out_ref):
    totals, source = head_tables(rate_ref, step_ref)
    out_ref[0] = totals
    out_ref[1] = jnp.transpose(source)
    s, t = places((LIVE, ROWS))
    live = live_count(kept_ref, sends_ref)
    out_ref[2, :LIVE] = row_mask(live, doc_ref, t, s)
    out_ref[2, LIVE:] = jnp.zeros((ROWS - LIVE, ROWS), F32)
    out_ref[3, :LIVE] = jnp.where(s < live, 1.0, 0.0)
    out_ref[3, LIVE:] = jnp.zeros((ROWS - LIVE, ROWS), F32)


def tables_call(kept, sends, rate, docs, steps):
    vmem = pl.BlockSpec(memory_space=pltpu.VMEM)
    return pl.pallas_call(
        tables_kernel,
        out_shape=pltpu.HBM((4, ROWS, ROWS), F32),
        in_specs=[vmem] * 5,
        out_specs=vmem,
        compiler_params=params(),
        cost_estimate=pl.CostEstimate(flops=0, bytes_accessed=2**19, transcendentals=HEADS * ROWS),
        name="tables",
    )(kept, sends, rate, docs, steps)


def scan_grad_kernel(skip_ref, tables_ref, g_ref, b_ref, *refs):
    step = pl.program_id(0)
    proj_refs, (out_ref, source_scr) = refs[:MEMBERS], refs[MEMBERS:]

    @pl.when(step == 0)
    def _():
        source = tables_ref[1]
        for k in range(GROUPS):
            source_scr[k] = pltpu.roll(source, HEADS - k * HPG, 1) if k else source

    bias = tables_ref[2, :LIVE, :]
    alive = tables_ref[3, :LIVE, :]
    half = lax.broadcasted_iota(jnp.int32, (ROWS, 128), 1) < HDIM
    out_ref[LIVE:, :] = jnp.zeros((ROWS - LIVE, SCAN_STEP * HPG * HDIM), BF16)
    for k in range(SCAN_STEP):
        q = step * SCAN_STEP + k
        totals = tables_ref[0, group_rows(q), :]
        source_col = source_scr[q]
        columns = slice(k * STATE, (k + 1) * STATE)
        c_proj = proj_refs[0][:, columns].astype(F32)
        for proj_ref in proj_refs[1:]:
            c_proj = c_proj + proj_ref[:, columns].astype(F32)
        c_proj = jnp.concatenate([c_proj.astype(BF16), jnp.zeros((ROWS - LIVE, STATE), BF16)], axis=0)
        affinity = lax.dot_general(
            b_ref[:LIVE, columns], c_proj, (((1,), (1,)), ((), ())), preferred_element_type=F32
        )
        for p in range(HPG // 2):
            lanes = slice(k * HPG * HDIM + p * 128, k * HPG * HDIM + p * 128 + 128)
            g_pair = g_ref[:, lanes]
            zero = jnp.zeros_like(g_pair)
            both = jnp.concatenate([jnp.where(half, g_pair, zero), jnp.where(half, zero, g_pair)], axis=0)
            kernels = []
            for i in range(2):
                h = 2 * p + i
                gap = (source_col[:LIVE, h : h + 1] - totals[h : h + 1, :]) + bias
                kernels.append((jnp.exp2(gap) * affinity).astype(BF16))
            grads = jnp.dot(jnp.concatenate(kernels, axis=1), both, preferred_element_type=F32)
            first = q * HPG + 2 * p
            gain = jnp.where(half[:LIVE], skip_ref[first], skip_ref[first + 1]) * alive
            grads = grads + gain * g_pair[:LIVE].astype(F32)
            out_ref[:LIVE, lanes] = grads.astype(BF16)


def scan_grad_call(skip, tables, out_grad, b_factors, shares):
    wide, narrow = SCAN_STEP * HPG * HDIM, SCAN_STEP * STATE
    return pl.pallas_call(
        scan_grad_kernel,
        grid=(GROUPS // SCAN_STEP,),
        out_shape=jax.ShapeDtypeStruct((ROWS, D), BF16),
        in_specs=[
            smem(),
            pl.BlockSpec((4, ROWS, ROWS), lambda q: (0, 0, 0)),
            pl.BlockSpec((ROWS, wide), lambda q: (0, q)),
            pl.BlockSpec((ROWS, narrow), lambda q: (0, q)),
        ]
        + [pl.BlockSpec((LIVE, narrow), lambda q: (0, q))] * MEMBERS,
        out_specs=pl.BlockSpec((ROWS, wide), lambda q: (0, q)),
        scratch_shapes=[pltpu.VMEM((GROUPS, ROWS, HEADS), F32)],
        compiler_params=params(),
        cost_estimate=pl.CostEstimate(
            flops=4 * LIVE * ROWS * D, bytes_accessed=4 * ROWS * D, transcendentals=HEADS * LIVE * ROWS
        ),
        name="scan_grad",
    )(skip, tables, out_grad, b_factors, *shares)


def weight_kernel(s_ref, *refs):
    c_refs, (keep_ref, send_ref, grads) = refs[:MEMBERS], refs[MEMBERS:]
    for c_ref, f in zip(c_refs, rows_at(-1)):
        grads[f] = c_ref[...]
    at = coordinates()
    first_core = at["core"] == 0

    def place(b, j):
        step = (j % 4 + 4 - at["x"]) % 4
        away = jnp.where(step == 0, AWAY[0], jnp.where(step == 1, AWAY[1], jnp.where(step == 2, AWAY[2], AWAY[3])))
        z = 2 * at["x"] + 1 + away if b else 2 * at["x"] + 8 - away
        return j // 4 * 8 + z % 8

    wide = 256
    rows = MEMBERS * LIVE
    for i in range(CHUNK // wide):
        part = lax.dot_general(
            s_ref[:, :, i * wide : (i + 1) * wide].reshape(rows, wide),
            grads[...].reshape(rows, NARROW),
            (((0,), (0,)), ((), ())),
            preferred_element_type=F32,
        ).reshape(8, 32, NARROW)
        b, core = i // 2, i % 2

        @pl.when(first_core == (core == 0))
        def _():
            for j in range(8):
                keep_ref[place(b, j)] = part[j]

        @pl.when(first_core != (core == 0))
        def _():
            for j in range(8):
                send_ref[place(b, j)] = part[j].astype(BF16)


def weight_call(pieces, grads):
    vmem = pl.BlockSpec(memory_space=pltpu.VMEM)
    return pl.pallas_call(
        weight_kernel,
        out_shape=[jax.ShapeDtypeStruct((16, 32, NARROW), kind) for kind in (F32, BF16)]
        + [jax.ShapeDtypeStruct((MEMBERS, LIVE, NARROW), BF16)],
        in_specs=[vmem] * 9,
        out_specs=[vmem] * 3,
        compiler_params=params(24 * 2**20),
        cost_estimate=pl.CostEstimate(
            flops=2 * MEMBERS * LIVE * CHUNK * NARROW, bytes_accessed=5 * 2**20, transcendentals=0
        ),
        name="weight_part",
    )(pieces, *grads)


def c_proj_kernel(w_ref, s_ref, out_ref):
    rows = MEMBERS * LIVE
    part = jnp.dot(s_ref[...].reshape(rows, CHUNK), w_ref[...], preferred_element_type=F32)
    out_ref[...] = part.astype(BF16).reshape(MEMBERS, LIVE, NARROW)


def c_proj_call(weights, pieces):
    vmem = pl.BlockSpec(memory_space=pltpu.VMEM)
    return pl.pallas_call(
        c_proj_kernel,
        out_shape=jax.ShapeDtypeStruct((MEMBERS, LIVE, NARROW), BF16),
        in_specs=[vmem] * 2,
        out_specs=vmem,
        compiler_params=params(24 * 2**20),
        cost_estimate=pl.CostEstimate(
            flops=2 * MEMBERS * LIVE * CHUNK * NARROW, bytes_accessed=4 * 2**20, transcendentals=0
        ),
        name="c_proj",
    )(weights, pieces)


def project_kernel(w_ref, proj_ref, grads, *refs):
    out_refs, half_refs, (top_ref, held, sems) = refs[: MEMBERS - 1], refs[MEMBERS - 1 : MEMBERS + 1], refs[MEMBERS + 1 :]
    rows = MEMBERS * LIVE
    wide = 256
    dests = rows_at(1)
    last_sems = [sems.at[k, MEMBERS - 1] for k in range(2)]
    halves = [
        pltpu.make_async_copy(
            held.at[dests[-1], :, pl.ds(k * HALF, HALF)], half_refs[k], last_sems[k]
        )
        for k in range(2)
    ]
    copies = []
    for k, (first, last) in enumerate(((0, NARROW + CHUNK // 2), (NARROW + CHUNK // 2, BOTH))):
        columns = pl.ds(first, last - first)
        copies.append(
            [
                pltpu.make_async_copy(held.at[f, :, columns], ref.at[:, columns], sems.at[k, i])
                for i, (ref, f) in enumerate(zip(out_refs, dests))
            ]
            + halves[k : k + 1]
        )
    held[:, :, :NARROW] = proj_ref[...]
    top = jnp.zeros((8, wide), F32)
    steps = CHUNK // wide
    for i in range(steps):
        part = lax.dot_general(
            grads[...].reshape(rows, NARROW),
            w_ref[i * wide : (i + 1) * wide, :],
            (((1,), (1,)), ((), ())),
            preferred_element_type=F32,
        )
        held[:, :, NARROW + i * wide : NARROW + (i + 1) * wide] = part.astype(BF16).reshape(
            MEMBERS, LIVE, wide
        )
        top = jnp.maximum(top, jnp.max(jnp.abs(part).reshape(rows // 8, 8, wide), axis=0))
        if i % (steps // 2) == steps // 2 - 1:
            for copy in copies[i // (steps // 2)]:
                copy.start()
    top_ref[...] = jnp.broadcast_to(jnp.max(top), (1, 128))
    for copy in copies[0] + copies[1]:
        copy.wait()


def project_call(weights, proj, grads):
    vmem = pl.BlockSpec(memory_space=pltpu.VMEM)
    out = pl.pallas_call(
        project_kernel,
        out_shape=[pltpu.VMEM((LIVE, BOTH), BF16)]
        + [pltpu.HBM((LIVE, BOTH), BF16)] * (MEMBERS - 2)
        + [pltpu.HBM((LIVE, HALF), BF16)] * 2
        + [jax.ShapeDtypeStruct((1, 128), F32)],
        in_specs=[vmem] * 3,
        out_specs=[pl.BlockSpec(memory_space=pl.ANY)] * (MEMBERS + 1) + [vmem],
        scratch_shapes=[
            pltpu.VMEM((MEMBERS, LIVE, BOTH), BF16),
            pltpu.SemaphoreType.DMA((2, MEMBERS)),
        ],
        compiler_params=params(24 * 2**20),
        cost_estimate=pl.CostEstimate(
            flops=2 * MEMBERS * LIVE * CHUNK * NARROW, bytes_accessed=6 * 2**20, transcendentals=0
        ),
        name="project",
    )(weights, proj, grads)
    return out[: MEMBERS + 1], out[MEMBERS + 1]


def peak_kernel(parts_ref, top_ref, sum_ref, tops_ref):
    total = parts_ref[0].astype(F32)
    for i in range(1, 16):
        total = total + parts_ref[i].astype(F32)
    sum_ref[...] = total
    lane = lax.broadcasted_iota(jnp.int32, (1, 128), 1)
    both = jnp.where(lane < 64, top_ref[...], jnp.max(jnp.abs(total)))
    tops_ref[...] = jnp.broadcast_to(both[None], (256, 1, 128))


def peak_call(parts, top):
    vmem = pl.BlockSpec(memory_space=pltpu.VMEM)
    return pl.pallas_call(
        peak_kernel,
        out_shape=[
            jax.ShapeDtypeStruct((32, NARROW), F32),
            jax.ShapeDtypeStruct((256, 1, 128), F32),
        ],
        in_specs=[vmem, vmem],
        out_specs=[vmem, vmem],
        compiler_params=params(16 * 2**20),
        cost_estimate=pl.CostEstimate(flops=16 * 32 * NARROW, bytes_accessed=2**20, transcendentals=0),
        name="peaks",
    )(parts, top)


def finish_kernel(tops_ref, sum_ref, *refs):
    back_refs, (input_ref, weight_ref, held, sems) = refs[: MEMBERS + 1], refs[MEMBERS + 1 :]
    split = HALF - NARROW
    tops = jnp.max(tops_ref[...], axis=0)
    scale = 1.0 / (tops[:, :1] + peak_eps)
    held[:, LIVE:, :] = jnp.zeros((MEMBERS, ROWS - LIVE, CHUNK), BF16)
    copies = []
    for i, (ref, f) in enumerate(zip(back_refs, rows_at(-1))):
        if i < MEMBERS - 1:
            held[i, :LIVE] = (ref[:, NARROW:].astype(F32) * scale).astype(BF16)
        else:
            held[i, :LIVE, :split] = (ref[:, NARROW:].astype(F32) * scale).astype(BF16)
            held[i, :LIVE, split:] = (back_refs[MEMBERS][...].astype(F32) * scale).astype(BF16)
        columns = pl.ds(pl.multiple_of(f * CHUNK, CHUNK), CHUNK)
        copies.append(pltpu.make_async_copy(held.at[i], input_ref.at[:, columns], sems.at[i]))
        copies[-1].start()
    weight_ref[...] = sum_ref[...] / (tops[:, 64:65] + peak_eps)
    for copy in copies:
        copy.wait()


def finish_call(tops, both, weight_sum):
    vmem = pl.BlockSpec(memory_space=pltpu.VMEM)
    return pl.pallas_call(
        finish_kernel,
        out_shape=[
            jax.ShapeDtypeStruct((ROWS, D), BF16),
            jax.ShapeDtypeStruct((32, NARROW), F32),
        ],
        in_specs=[vmem] * (3 + MEMBERS),
        out_specs=[pl.BlockSpec(memory_space=pl.ANY), vmem],
        scratch_shapes=[
            pltpu.VMEM((MEMBERS, ROWS, CHUNK), BF16),
            pltpu.SemaphoreType.DMA((MEMBERS,)),
        ],
        compiler_params=params(16 * 2**20),
        cost_estimate=pl.CostEstimate(flops=LIVE * D, bytes_accessed=4 * ROWS * D, transcendentals=0),
        name="finish",
    )(tops, weight_sum, *both)


def shards(
    section_input,
    c_weight,
    scan_input,
    b_factors,
    step_size,
    decay_rate,
    skip_gain,
    out_grad,
    doc_index,
    kept_rows,
    send_counts,
):
    kept = kept_rows.reshape(1, 32)
    sends = send_counts.reshape(32, 32)
    rate, docs = decay_rate.reshape(1, HEADS), doc_index.reshape(1, ROWS)

    pieces = exchange(pack(section_input), WIDE)

    c_own = c_grad_call(kept, sends, rate, docs, step_size, out_grad, scan_input, b_factors)
    grads = [c_own] + [lax.ppermute(c_own, ALL, moved(*step)) for step in STEPS[1:]]

    steps, c_own = lax.optimization_barrier((step_size, c_own))
    tables = tables_call(kept, sends, rate, docs, steps)
    proj = c_proj_call(c_weight, pieces)
    grads, tables, proj = lax.optimization_barrier((grads, tables, proj))
    keep, send, grads = weight_call(pieces, grads)
    both, top = project_call(c_weight, proj, grads)
    got = to_core(send)
    got, top = lax.optimization_barrier((got, top))
    parts = (keep + got.astype(F32)).astype(BF16)
    parts = lax.all_to_all(parts, "dp", 0, 0, axis_index_groups=SAME_CORE)

    back = [both[0]] + [lax.ppermute(both[i], ALL, moved(*STEPS[i])) for i in range(1, 7)]
    weight_sum, tops = peak_call(parts, top)
    weight_sum, *late = lax.optimization_barrier((weight_sum, *both[7:]))
    tops = exchange(tops, None)
    back += [lax.ppermute(value, ALL, moved(*STEPS[7])) for value in late]
    weight_sum = lax.ppermute(weight_sum, ALL, HOME)
    both = [pltpu.with_memory_space_constraint(value, pltpu.VMEM) for value in back]
    scan_grad = scan_grad_call(skip_gain, tables, out_grad, b_factors, both[:MEMBERS])
    input_grad, readout_weight_gradient = finish_call(tops, both, weight_sum)
    return (input_grad, scan_grad, readout_weight_gradient)


def solution(mesh):
    rows = P(ALL, None)
    placed = (
        rows,
        P("fsdp", None),
        rows,
        rows,
        P(None, ALL),
        P(),
        P(),
        rows,
        P(ALL),
        P(None, "fsdp"),
        P(None, "fsdp", None),
    )
    return jax.shard_map(
        shards, mesh=mesh, in_specs=placed, out_specs=(rows, rows, rows), check_vma=False
    )
```

```python
import jax
import jax.numpy as jnp
from jax import lax
from jax.experimental import pallas as pl
from jax.experimental.pallas import tpu as pltpu
from jax.sharding import PartitionSpec as P

GROUPS = 4
STATE = 128
HEADS = 128
HDIM = 64
HPG = HEADS // GROUPS
ROWS = 128
LIVE = 96
D = 8192
NARROW = GROUPS * STATE
MEMBERS = 8
CHUNK = D // MEMBERS
BOTH = NARROW + CHUNK
HALF = BOTH // 2
VMEM_LIMIT = 60 * 2**20
C_STEP = 4
SCAN_STEP = 2
LOG2E = 1.4426950408889634
ALL = ("dp", "fsdp")
peak_eps = 1e-06
F32 = jnp.float32
BF16 = jnp.bfloat16


def joint(y_hi, x, y_lo, z, core):
    return (y_lo * 16 + z * 2 + core) * 8 + y_hi * 4 + x


WIDE = [
    [joint(h, x, h ^ s, z, c) for h in (0, 1) for x in range(4)]
    for s in (0, 1)
    for z in range(8)
    for c in (0, 1)
]
def moved(dx, pair):
    return [
        (joint(h, x, l, z, c), joint(h ^ pair, (x + dx) % 4, l ^ pair, z, c))
        for h in (0, 1)
        for x in range(4)
        for l in (0, 1)
        for z in range(8)
        for c in (0, 1)
    ]


STEPS = [(0, 0), (2, 1), (2, 0), (1, 1), (3, 1), (0, 1), (1, 0), (3, 0)]
C_ORDER = (0, 5, 2, 1, 3, 4, 6, 7)
CORE_SWAP = [(i, i ^ 1) for i in range(32)]
SAME_CORE = [[l * 16 + z * 2 + c for l in (0, 1) for z in range(8)] for c in (0, 1)]
AWAY = (3, 2, 0, 1)


def summed_at(x, b, x_home):
    away = AWAY[(x_home - x) % 4]
    return (2 * x + 1 + away) % 8 if b else (2 * x - away) % 8


HOME = [
    (joint(h, x, k, summed_at(x, b, i), c), joint(k, i, h, 2 * x + b, c))
    for h in (0, 1)
    for x in range(4)
    for k in (0, 1)
    for i in range(4)
    for b in (0, 1)
    for c in (0, 1)
]


def exchange(value, groups):
    return lax.all_to_all(value, ALL, 0, 0, axis_index_groups=groups)


def to_core(value):
    return lax.ppermute(value, "dp", CORE_SWAP)


def coordinates():
    dp, f = lax.axis_index("dp"), lax.axis_index("fsdp")
    return dict(dp=dp, core=dp % 2, y_lo=dp // 16, x=f % 4, y_hi=f // 4)


def rows_at(sign):
    at = coordinates()
    return [(at["y_hi"] + pair) % 2 * 4 + (at["x"] + 4 + sign * dx) % 4 for dx, pair in STEPS]


def params(limit=VMEM_LIMIT):
    return pltpu.CompilerParams(vmem_limit_bytes=limit)


def pack_kernel(s_ref, wide_ref, sems):
    copies = [
        pltpu.make_async_copy(
            s_ref.at[pl.ds(0, LIVE), pl.ds(f * CHUNK, CHUNK)], wide_ref.at[f], sems.at[f]
        )
        for f in range(MEMBERS)
    ]
    for copy in copies:
        copy.start()
    for copy in copies:
        copy.wait()


def pack(section_input):
    return pl.pallas_call(
        pack_kernel,
        out_shape=jax.ShapeDtypeStruct((MEMBERS, LIVE, CHUNK), BF16),
        in_specs=[pl.BlockSpec(memory_space=pl.ANY)],
        out_specs=pl.BlockSpec(memory_space=pltpu.VMEM),
        scratch_shapes=[pltpu.SemaphoreType.DMA((MEMBERS,))],
        compiler_params=params(),
        cost_estimate=pl.CostEstimate(flops=0, bytes_accessed=4 * LIVE * D, transcendentals=0),
        name="pack",
    )(section_input)


def live_count(kept_ref, sends_ref):
    dp = coordinates()["dp"]
    row, column = (lax.broadcasted_iota(jnp.int32, (32, 32), k) for k in range(2))
    counts = jnp.where(row == dp, sends_ref[...], 0) + jnp.where(
        (row == 0) & (column == dp), kept_ref[...], 0
    )
    counts = jnp.sum(counts.astype(F32), axis=0, keepdims=True)
    return jnp.sum(counts, axis=1, keepdims=True)


def places(shape):
    rows = [lax.broadcasted_iota(jnp.int32, shape, k).astype(F32) for k in range(2)]
    return rows


def head_tables(rate_ref, step_ref):
    steps = step_ref[...]
    totals = steps * jnp.transpose(jnp.broadcast_to(rate_ref[...], (HEADS, HEADS)))
    lane = lax.broadcasted_iota(jnp.int32, totals.shape, 1)
    reach = 1
    while reach < ROWS:
        totals = totals + jnp.where(lane >= reach, pltpu.roll(totals, reach, 1), 0.0)
        reach *= 2
    totals = totals * LOG2E
    return totals, totals + jnp.log(steps) * LOG2E


def keep_tables(along_ref, down_ref, along, down):
    along_ref[...] = along
    down = jnp.transpose(down)
    for q in range(GROUPS):
        down_ref[q] = pltpu.roll(down, HEADS - q * HPG, 1) if q else down


def row_mask(live, doc_ref, target, source):
    along = jnp.broadcast_to(doc_ref[...].astype(F32), (ROWS, ROWS))
    down = jnp.transpose(along)
    keep = (along[:LIVE] == down[:LIVE]) & (source <= target) & (target < live) & (source < live)
    return jnp.where(keep, 0.0, -1e30).astype(F32)


def group_rows(q):
    return pl.ds(pl.multiple_of(q * HPG, HPG), HPG)


def c_grad_kernel(
    kept_ref, sends_ref, rate_ref, doc_ref, step_ref, g_ref, x_ref, b_ref, out_ref, source_scr, totals_scr, bias_scr
):
    step = pl.program_id(0)

    @pl.when(step == 0)
    def _():
        totals, source = head_tables(rate_ref, step_ref)
        keep_tables(source_scr, totals_scr, source, totals)
        t, s = places((LIVE, ROWS))
        bias_scr[...] = row_mask(live_count(kept_ref, sends_ref), doc_ref, t, s)

    bias = bias_scr[...]
    upper = lax.broadcasted_iota(jnp.int32, (128, ROWS), 0) < HDIM
    for k in range(C_STEP):
        q = step * C_STEP + k
        source = source_scr[group_rows(q), :]
        totals_col = totals_scr[q]
        mixing = jnp.zeros((LIVE, ROWS), F32)
        for p in range(HPG // 2):
            lanes = slice(k * HPG * HDIM + p * 128, k * HPG * HDIM + p * 128 + 128)
            x_pair = x_ref[:, lanes]
            zero = jnp.zeros_like(x_pair)
            x_turned = jnp.transpose(x_pair)
            both = jnp.concatenate([jnp.where(upper, x_turned, zero), jnp.where(upper, zero, x_turned)], axis=1)
            inner = jnp.dot(g_ref[:, lanes], both, preferred_element_type=F32)
            for i in range(2):
                h = 2 * p + i
                gap = (source[h : h + 1, :] - totals_col[:LIVE, h : h + 1]) + bias
                mixing = mixing + jnp.exp2(gap) * inner[:, i * 128 : i * 128 + 128]
        columns = slice(k * STATE, (k + 1) * STATE)
        out_ref[:, columns] = jnp.dot(
            mixing.astype(BF16), b_ref[:, columns], preferred_element_type=F32
        ).astype(BF16)


def smem():
    return pl.BlockSpec(memory_space=pltpu.SMEM)


def row_spec():
    return pl.BlockSpec((1, 128), lambda q: (0, 0))


def c_grad_call(kept, sends, rate, docs, steps, out_grad, scan_input, b_factors):
    wide, narrow = C_STEP * HPG * HDIM, C_STEP * STATE
    return pl.pallas_call(
        c_grad_kernel,
        grid=(GROUPS // C_STEP,),
        out_shape=pltpu.VMEM((LIVE, NARROW), BF16),
        in_specs=[
            pl.BlockSpec((1, 32), lambda q: (0, 0)),
            pl.BlockSpec((32, 32), lambda q: (0, 0)),
            row_spec(),
            row_spec(),
            pl.BlockSpec((HEADS, ROWS), lambda q: (0, 0)),
            pl.BlockSpec((LIVE, wide), lambda q: (0, q)),
            pl.BlockSpec((ROWS, wide), lambda q: (0, q)),
            pl.BlockSpec((ROWS, narrow), lambda q: (0, q)),
        ],
        out_specs=pl.BlockSpec((LIVE, narrow), lambda q: (0, q)),
        scratch_shapes=[
            pltpu.VMEM((HEADS, ROWS), F32),
            pltpu.VMEM((GROUPS, ROWS, HEADS), F32),
            pltpu.VMEM((LIVE, ROWS), F32),
        ],
        compiler_params=params(),
        cost_estimate=pl.CostEstimate(
            flops=4 * LIVE * ROWS * D, bytes_accessed=4 * ROWS * D, transcendentals=HEADS * LIVE * ROWS
        ),
        name="c_grad",
    )(kept, sends, rate, docs, steps, out_grad, scan_input, b_factors)


def tables_kernel(kept_ref, sends_ref, rate_ref, doc_ref, step_ref, out_ref):
    totals, source = head_tables(rate_ref, step_ref)
    out_ref[0] = totals
    out_ref[1] = jnp.transpose(source)
    s, t = places((LIVE, ROWS))
    live = live_count(kept_ref, sends_ref)
    out_ref[2, :LIVE] = row_mask(live, doc_ref, t, s)
    out_ref[2, LIVE:] = jnp.zeros((ROWS - LIVE, ROWS), F32)
    out_ref[3, :LIVE] = jnp.where(s < live, 1.0, 0.0)
    out_ref[3, LIVE:] = jnp.zeros((ROWS - LIVE, ROWS), F32)


def tables_call(kept, sends, rate, docs, steps):
    vmem = pl.BlockSpec(memory_space=pltpu.VMEM)
    return pl.pallas_call(
        tables_kernel,
        out_shape=pltpu.HBM((4, ROWS, ROWS), F32),
        in_specs=[vmem] * 5,
        out_specs=vmem,
        compiler_params=params(),
        cost_estimate=pl.CostEstimate(flops=0, bytes_accessed=2**19, transcendentals=HEADS * ROWS),
        name="tables",
    )(kept, sends, rate, docs, steps)


def scan_grad_kernel(skip_ref, tables_ref, g_ref, b_ref, *refs):
    step = pl.program_id(0)
    proj_refs, (out_ref, source_scr) = refs[:MEMBERS], refs[MEMBERS:]

    @pl.when(step == 0)
    def _():
        source = tables_ref[1]
        for k in range(GROUPS):
            source_scr[k] = pltpu.roll(source, HEADS - k * HPG, 1) if k else source

    bias = tables_ref[2, :LIVE, :]
    alive = tables_ref[3, :LIVE, :]
    half = lax.broadcasted_iota(jnp.int32, (ROWS, 128), 1) < HDIM
    out_ref[LIVE:, :] = jnp.zeros((ROWS - LIVE, SCAN_STEP * HPG * HDIM), BF16)
    for k in range(SCAN_STEP):
        q = step * SCAN_STEP + k
        totals = tables_ref[0, group_rows(q), :]
        source_col = source_scr[q]
        columns = slice(k * STATE, (k + 1) * STATE)
        c_proj = proj_refs[0][:, columns].astype(F32)
        for proj_ref in proj_refs[1:]:
            c_proj = c_proj + proj_ref[:, columns].astype(F32)
        c_proj = jnp.concatenate([c_proj.astype(BF16), jnp.zeros((ROWS - LIVE, STATE), BF16)], axis=0)
        affinity = lax.dot_general(
            b_ref[:LIVE, columns], c_proj, (((1,), (1,)), ((), ())), preferred_element_type=F32
        )
        for p in range(HPG // 2):
            lanes = slice(k * HPG * HDIM + p * 128, k * HPG * HDIM + p * 128 + 128)
            g_pair = g_ref[:, lanes]
            zero = jnp.zeros_like(g_pair)
            both = jnp.concatenate([jnp.where(half, g_pair, zero), jnp.where(half, zero, g_pair)], axis=0)
            kernels = []
            for i in range(2):
                h = 2 * p + i
                gap = (source_col[:LIVE, h : h + 1] - totals[h : h + 1, :]) + bias
                kernels.append((jnp.exp2(gap) * affinity).astype(BF16))
            grads = jnp.dot(jnp.concatenate(kernels, axis=1), both, preferred_element_type=F32)
            first = q * HPG + 2 * p
            gain = jnp.where(half[:LIVE], skip_ref[first], skip_ref[first + 1]) * alive
            grads = grads + gain * g_pair[:LIVE].astype(F32)
            out_ref[:LIVE, lanes] = grads.astype(BF16)


def scan_grad_call(skip, tables, out_grad, b_factors, shares):
    wide, narrow = SCAN_STEP * HPG * HDIM, SCAN_STEP * STATE
    return pl.pallas_call(
        scan_grad_kernel,
        grid=(GROUPS // SCAN_STEP,),
        out_shape=jax.ShapeDtypeStruct((ROWS, D), BF16),
        in_specs=[
            smem(),
            pl.BlockSpec((4, ROWS, ROWS), lambda q: (0, 0, 0)),
            pl.BlockSpec((ROWS, wide), lambda q: (0, q)),
            pl.BlockSpec((ROWS, narrow), lambda q: (0, q)),
        ]
        + [pl.BlockSpec((LIVE, narrow), lambda q: (0, q))] * MEMBERS,
        out_specs=pl.BlockSpec((ROWS, wide), lambda q: (0, q)),
        scratch_shapes=[pltpu.VMEM((GROUPS, ROWS, HEADS), F32)],
        compiler_params=params(),
        cost_estimate=pl.CostEstimate(
            flops=4 * LIVE * ROWS * D, bytes_accessed=4 * ROWS * D, transcendentals=HEADS * LIVE * ROWS
        ),
        name="scan_grad",
    )(skip, tables, out_grad, b_factors, *shares)


def weight_kernel(s_ref, *refs):
    c_refs, (keep_ref, send_ref, grads) = refs[:MEMBERS], refs[MEMBERS:]
    rows = rows_at(-1)
    for c_ref, i in zip(c_refs, C_ORDER):
        grads[rows[i]] = c_ref[...]
    at = coordinates()
    first_core = at["core"] == 0

    def place(b, j):
        step = (j % 4 + 4 - at["x"]) % 4
        away = jnp.where(step == 0, AWAY[0], jnp.where(step == 1, AWAY[1], jnp.where(step == 2, AWAY[2], AWAY[3])))
        z = 2 * at["x"] + 1 + away if b else 2 * at["x"] + 8 - away
        return j // 4 * 8 + z % 8

    wide = 256
    rows = MEMBERS * LIVE
    for i in range(CHUNK // wide):
        part = lax.dot_general(
            s_ref[:, :, i * wide : (i + 1) * wide].reshape(rows, wide),
            grads[...].reshape(rows, NARROW),
            (((0,), (0,)), ((), ())),
            preferred_element_type=F32,
        ).reshape(8, 32, NARROW)
        b, core = i // 2, i % 2

        @pl.when(first_core == (core == 0))
        def _():
            for j in range(8):
                keep_ref[place(b, j)] = part[j]

        @pl.when(first_core != (core == 0))
        def _():
            for j in range(8):
                send_ref[place(b, j)] = part[j].astype(BF16)


def weight_call(pieces, grads):
    vmem = pl.BlockSpec(memory_space=pltpu.VMEM)
    return pl.pallas_call(
        weight_kernel,
        out_shape=[jax.ShapeDtypeStruct((16, 32, NARROW), kind) for kind in (F32, BF16)]
        + [jax.ShapeDtypeStruct((MEMBERS, LIVE, NARROW), BF16)],
        in_specs=[vmem] * 9,
        out_specs=[vmem] * 3,
        compiler_params=params(24 * 2**20),
        cost_estimate=pl.CostEstimate(
            flops=2 * MEMBERS * LIVE * CHUNK * NARROW, bytes_accessed=5 * 2**20, transcendentals=0
        ),
        name="weight_part",
    )(pieces, *grads)


def c_proj_kernel(w_ref, s_ref, out_ref):
    rows = MEMBERS * LIVE
    part = jnp.dot(s_ref[...].reshape(rows, CHUNK), w_ref[...], preferred_element_type=F32)
    out_ref[...] = part.astype(BF16).reshape(MEMBERS, LIVE, NARROW)


def c_proj_call(weights, pieces):
    vmem = pl.BlockSpec(memory_space=pltpu.VMEM)
    return pl.pallas_call(
        c_proj_kernel,
        out_shape=jax.ShapeDtypeStruct((MEMBERS, LIVE, NARROW), BF16),
        in_specs=[vmem] * 2,
        out_specs=vmem,
        compiler_params=params(24 * 2**20),
        cost_estimate=pl.CostEstimate(
            flops=2 * MEMBERS * LIVE * CHUNK * NARROW, bytes_accessed=4 * 2**20, transcendentals=0
        ),
        name="c_proj",
    )(weights, pieces)


def project_kernel(w_ref, proj_ref, grads, *refs):
    out_refs, half_refs, (top_ref, held, sems) = refs[: MEMBERS - 1], refs[MEMBERS - 1 : MEMBERS + 1], refs[MEMBERS + 1 :]
    rows = MEMBERS * LIVE
    wide = 256
    dests = rows_at(1)
    last_sems = [sems.at[k, MEMBERS - 1] for k in range(2)]
    halves = [
        pltpu.make_async_copy(
            held.at[dests[-1], :, pl.ds(k * HALF, HALF)], half_refs[k], last_sems[k]
        )
        for k in range(2)
    ]
    copies = []
    for k, (first, last) in enumerate(((0, NARROW + CHUNK // 2), (NARROW + CHUNK // 2, BOTH))):
        columns = pl.ds(first, last - first)
        copies.append(
            [
                pltpu.make_async_copy(held.at[f, :, columns], ref.at[:, columns], sems.at[k, i])
                for i, (ref, f) in enumerate(zip(out_refs, dests))
            ]
            + halves[k : k + 1]
        )
    held[:, :, :NARROW] = proj_ref[...]
    top = jnp.zeros((8, wide), F32)
    steps = CHUNK // wide
    for i in range(steps):
        part = lax.dot_general(
            grads[...].reshape(rows, NARROW),
            w_ref[i * wide : (i + 1) * wide, :],
            (((1,), (1,)), ((), ())),
            preferred_element_type=F32,
        )
        held[:, :, NARROW + i * wide : NARROW + (i + 1) * wide] = part.astype(BF16).reshape(
            MEMBERS, LIVE, wide
        )
        top = jnp.maximum(top, jnp.max(jnp.abs(part).reshape(rows // 8, 8, wide), axis=0))
        if i % (steps // 2) == steps // 2 - 1:
            for copy in copies[i // (steps // 2)]:
                copy.start()
    top_ref[...] = jnp.broadcast_to(jnp.max(top), (1, 128))
    for copy in copies[0] + copies[1]:
        copy.wait()


def project_call(weights, proj, grads):
    vmem = pl.BlockSpec(memory_space=pltpu.VMEM)
    out = pl.pallas_call(
        project_kernel,
        out_shape=[pltpu.VMEM((LIVE, BOTH), BF16)]
        + [pltpu.HBM((LIVE, BOTH), BF16)] * (MEMBERS - 2)
        + [pltpu.HBM((LIVE, HALF), BF16)] * 2
        + [jax.ShapeDtypeStruct((1, 128), F32)],
        in_specs=[vmem] * 3,
        out_specs=[pl.BlockSpec(memory_space=pl.ANY)] * (MEMBERS + 1) + [vmem],
        scratch_shapes=[
            pltpu.VMEM((MEMBERS, LIVE, BOTH), BF16),
            pltpu.SemaphoreType.DMA((2, MEMBERS)),
        ],
        compiler_params=params(24 * 2**20),
        cost_estimate=pl.CostEstimate(
            flops=2 * MEMBERS * LIVE * CHUNK * NARROW, bytes_accessed=6 * 2**20, transcendentals=0
        ),
        name="project",
    )(weights, proj, grads)
    return out[: MEMBERS + 1], out[MEMBERS + 1]


def peak_kernel(parts_ref, top_ref, sum_ref, tops_ref):
    total = parts_ref[0].astype(F32)
    for i in range(1, 16):
        total = total + parts_ref[i].astype(F32)
    sum_ref[...] = total
    lane = lax.broadcasted_iota(jnp.int32, (1, 128), 1)
    both = jnp.where(lane < 64, top_ref[...], jnp.max(jnp.abs(total)))
    tops_ref[...] = jnp.broadcast_to(both[None], (256, 1, 128))


def peak_call(parts, top):
    vmem = pl.BlockSpec(memory_space=pltpu.VMEM)
    return pl.pallas_call(
        peak_kernel,
        out_shape=[
            jax.ShapeDtypeStruct((32, NARROW), F32),
            jax.ShapeDtypeStruct((256, 1, 128), F32),
        ],
        in_specs=[vmem, vmem],
        out_specs=[vmem, vmem],
        compiler_params=params(16 * 2**20),
        cost_estimate=pl.CostEstimate(flops=16 * 32 * NARROW, bytes_accessed=2**20, transcendentals=0),
        name="peaks",
    )(parts, top)


def finish_kernel(tops_ref, sum_ref, *refs):
    back_refs, (input_ref, weight_ref, held, sems) = refs[: MEMBERS + 1], refs[MEMBERS + 1 :]
    split = HALF - NARROW
    tops = jnp.max(tops_ref[...], axis=0)
    scale = 1.0 / (tops[:, :1] + peak_eps)
    held[:, LIVE:, :] = jnp.zeros((MEMBERS, ROWS - LIVE, CHUNK), BF16)
    copies = []
    for i, (ref, f) in enumerate(zip(back_refs, rows_at(-1))):
        if i < MEMBERS - 1:
            held[i, :LIVE] = (ref[:, NARROW:].astype(F32) * scale).astype(BF16)
        else:
            held[i, :LIVE, :split] = (ref[:, NARROW:].astype(F32) * scale).astype(BF16)
            held[i, :LIVE, split:] = (back_refs[MEMBERS][...].astype(F32) * scale).astype(BF16)
        columns = pl.ds(pl.multiple_of(f * CHUNK, CHUNK), CHUNK)
        copies.append(pltpu.make_async_copy(held.at[i], input_ref.at[:, columns], sems.at[i]))
        copies[-1].start()
    weight_ref[...] = sum_ref[...] / (tops[:, 64:65] + peak_eps)
    for copy in copies:
        copy.wait()


def finish_call(tops, both, weight_sum):
    vmem = pl.BlockSpec(memory_space=pltpu.VMEM)
    return pl.pallas_call(
        finish_kernel,
        out_shape=[
            jax.ShapeDtypeStruct((ROWS, D), BF16),
            jax.ShapeDtypeStruct((32, NARROW), F32),
        ],
        in_specs=[vmem] * (3 + MEMBERS),
        out_specs=[pl.BlockSpec(memory_space=pl.ANY), vmem],
        scratch_shapes=[
            pltpu.VMEM((MEMBERS, ROWS, CHUNK), BF16),
            pltpu.SemaphoreType.DMA((MEMBERS,)),
        ],
        compiler_params=params(16 * 2**20),
        cost_estimate=pl.CostEstimate(flops=LIVE * D, bytes_accessed=4 * ROWS * D, transcendentals=0),
        name="finish",
    )(tops, weight_sum, *both)


def shards(
    section_input,
    c_weight,
    scan_input,
    b_factors,
    step_size,
    decay_rate,
    skip_gain,
    out_grad,
    doc_index,
    kept_rows,
    send_counts,
):
    kept = kept_rows.reshape(1, 32)
    sends = send_counts.reshape(32, 32)
    rate, docs = decay_rate.reshape(1, HEADS), doc_index.reshape(1, ROWS)

    pieces = exchange(pack(section_input), WIDE)

    c_own = c_grad_call(kept, sends, rate, docs, step_size, out_grad, scan_input, b_factors)
    grads = [c_own] + [lax.ppermute(c_own, ALL, moved(*step)) for step in STEPS[1:]]
    grads = [grads[i] for i in C_ORDER]

    steps, c_own = lax.optimization_barrier((step_size, c_own))
    tables = tables_call(kept, sends, rate, docs, steps)
    proj = c_proj_call(c_weight, pieces)
    grads, tables, proj = lax.optimization_barrier((grads, tables, proj))
    keep, send, grads = weight_call(pieces, grads)
    both, top = project_call(c_weight, proj, grads)
    got = to_core(send)
    got, top = lax.optimization_barrier((got, top))
    parts = (keep + got.astype(F32)).astype(BF16)
    parts = lax.all_to_all(parts, "dp", 0, 0, axis_index_groups=SAME_CORE)

    back = [both[0]] + [lax.ppermute(both[i], ALL, moved(*STEPS[i])) for i in range(1, 7)]
    weight_sum, tops = peak_call(parts, top)
    weight_sum, *late = lax.optimization_barrier((weight_sum, *both[7:]))
    tops = exchange(tops, None)
    back += [lax.ppermute(value, ALL, moved(*STEPS[7])) for value in late]
    weight_sum = lax.ppermute(weight_sum, ALL, HOME)
    both = [pltpu.with_memory_space_constraint(value, pltpu.VMEM) for value in back]
    scan_grad = scan_grad_call(skip_gain, tables, out_grad, b_factors, both[:MEMBERS])
    input_grad, readout_weight_gradient = finish_call(tops, both, weight_sum)
    return (input_grad, scan_grad, readout_weight_gradient)


def solution(mesh):
    rows = P(ALL, None)
    placed = (
        rows,
        P("fsdp", None),
        rows,
        rows,
        P(None, ALL),
        P(),
        P(),
        rows,
        P(ALL),
        P(None, "fsdp"),
        P(None, "fsdp", None),
    )
    return jax.shard_map(
        shards, mesh=mesh, in_specs=placed, out_specs=(rows, rows, rows), check_vma=False
    )
```
